32 devices in a mesh: shift: 4 (over x, core), rows: 8 (over z, y).
Axes of the slice: x: 2, y: 2, z: 4, core: 2. Of those that a mesh axis runs over, the one named last changes fastest.
Arguments:
- neighbours: int32 [64, 8], P('rows'), may hold values from 0 to 63, as said below
- couplings: float32 [64, 8, 128, 128], P('rows'), may hold values from -0.01953125 to 0.01953125
- eigvectors: float32 [64, 128, 128], P('rows'), may hold values from -1 to 1, as said below
- eigvalues: float32 [64, 128], P('rows'), may hold values from -2.5 to 2.5
- start_block: float32 [8192, 128], P('rows'), may hold values from -240 to 240
Outputs:
- basis: float32 [8192, 128], P('rows')
- basis_image: float32 [8192, 128], P('rows')
- projected: float32 [128, 128], replicated
The draws below stay inside these ranges and needn't reach their ends.
Inputs may be any that keep to these rules, and one draw needn't show every extreme that they name: Each block's 8 neighbours are distinct blocks other than itself, each within 8 blocks of it. `eigvectors`: each block's matrix has orthonormal columns up to rounding.
All inputs are finite; a program needn't handle non-finite values.
Results may differ from the reference program's by a relative error of at most 0.00025.
Values sent between devices are 32-bit elements; how exact they have to be, the bound alone decides.
No kernel may reach another device: no remote copies, remote signals or barrier semaphores. Data moves between devices by JAX's collectives and lax.ppermute only.
A program may use at most 64 MiB of HBM per device.

```python
import jax
import jax.numpy as jnp
from jax import lax

BLK = 128
NCOL = 128
NNB = 8
SWEEPS = 3
BLK_DEV = 8
NSHIFT = 4
NBLK = 64
NROWS = 8192


def draw_neighbours(key, part):
    offsets = jnp.concatenate([jnp.arange(-BLK_DEV, 0, dtype=jnp.int32), jnp.arange(1, BLK_DEV + 1, dtype=jnp.int32)])
    block_ids = jnp.arange(NBLK, dtype=jnp.int32)[:, None]
    candidates = block_ids + offsets[None, :]
    valid = (candidates >= 0) & (candidates < NBLK)
    scores = jax.random.randint(key, (NBLK, 2 * BLK_DEV), 0, 1 << 20, dtype=jnp.int32)
    scores = scores * (4 * BLK_DEV) + jnp.arange(2 * BLK_DEV, dtype=jnp.int32)[None, :]
    scores = jnp.where(valid, scores, (1 << 30) + jnp.arange(2 * BLK_DEV, dtype=jnp.int32)[None, :])
    order = jnp.argsort(scores, axis=1, stable=True)[:, :NNB]
    return jnp.take_along_axis(candidates, order, axis=1).astype(jnp.int32)


def draw_eigvectors(key, part):
    raw = jax.random.normal(key, (NBLK, BLK, BLK), jnp.float32)
    orthonormal, _ = jnp.linalg.qr(raw)
    return orthonormal.astype(jnp.float32)


def draw_start_block(key, part):
    key_a = jax.random.fold_in(key, 11)
    key_b = jax.random.fold_in(key, 12)
    key_c = jax.random.fold_in(key, 13)
    position = jnp.arange(NROWS, dtype=jnp.float32)[:, None] / NROWS
    rough = jax.random.uniform(key_b, (NROWS, 1), jnp.float32, 0.5, 1.5)
    row_scale = jnp.exp(jnp.log(10.0) * position) * rough
    col_scale = jnp.exp(jnp.log(4.0) * jax.random.uniform(key_c, (1, NCOL), jnp.float32))
    values = jnp.clip(jax.random.normal(key_a, (NROWS, NCOL), jnp.float32), -4.0, 4.0)
    return (values * row_scale * col_scale).astype(jnp.float32)


def steps_of(rng, extent, shards, least, largest):
    def one(dim, blocks):
        draws = jax.random.uniform(jax.random.fold_in(jax.random.fold_in(rng, 6), dim), (blocks,), jnp.float32, least / len(shards), largest / len(shards))
        return jnp.repeat(jnp.exp(draws), extent[dim] // blocks).reshape((-1,) + (1,) * (len(extent) - dim - 1))

    gain = one(*shards[0])
    for cut in shards[1:]:
        gain = gain * one(*cut)
    return gain


def gaussian(rng, extent, spread, bound, shards=(), held_as=jnp.bfloat16):
    gain = steps_of(rng, extent, shards, -0.22, 0.18) if shards else 1.0
    entries = jax.random.normal(rng, extent, jnp.float32) * spread * gain
    return jnp.minimum(jnp.maximum(entries, -bound), bound).astype(held_as)


def setup_inputs(seed: int = 0) -> dict:
    key_of = jax.random.split(jax.random.key(seed), 6)
    return {
        "neighbours": draw_neighbours(jax.random.fold_in(key_of[5], 71), 0),
        "couplings": gaussian(key_of[1], (NBLK, NNB, BLK, BLK), (625 * BLK) ** -0.5, 0.01953125, ((0, 8),), jnp.float32),
        "eigvectors": draw_eigvectors(jax.random.fold_in(key_of[5], 71), 0),
        "eigvalues": jnp.clip(jax.random.uniform(key_of[3], (NBLK, BLK), jnp.float32, -2.5, 2.5) * steps_of(key_of[3], (NBLK, BLK), ((0, 8),), -0.4, 0.0), -2.5, 2.5),
        "start_block": draw_start_block(jax.random.fold_in(key_of[5], 71), 0),
    }


radius = 1.0
damping = 0.8

def unrotate(vectors, field):
    return jnp.einsum('imn,imc->inc', vectors, field, precision=lax.Precision.HIGHEST)

def rotate(vectors, field):
    return jnp.einsum('inm,imc->inc', vectors, field, precision=lax.Precision.HIGHEST)

def shifted_inverse(vectors, values, field, real_part, imag_part):
    width = field.shape[-1] // 2
    spun = unrotate(vectors, field)
    offset = real_part - values
    denom = offset * offset + imag_part * imag_part
    scale_re = (offset / denom)[..., None]
    scale_im = (-imag_part / denom)[..., None]
    first = spun[..., :width]
    second = spun[..., width:]
    mixed = jnp.concatenate([scale_re * first - scale_im * second, scale_re * second + scale_im * first], axis=-1)
    return rotate(vectors, mixed)

def diagonal_part(vectors, values, field):
    return rotate(vectors, values[..., None] * unrotate(vectors, field))

def coupled(near_blocks, couplings):
    return jnp.einsum('iknm,ikmc->inc', couplings, near_blocks, precision=lax.Precision.HIGHEST)

def reference(neighbours, couplings, eigvectors, eigvalues, start_block):
    blocks_b = start_block.reshape(NBLK, BLK, NCOL)
    rhs = jnp.concatenate([blocks_b, jnp.zeros_like(blocks_b)], axis=-1)

    def operate(field):
        return diagonal_part(eigvectors, eigvalues, field) + coupled(field[neighbours], couplings)

    def contour_term(total, index):
        angle = jnp.pi * (index.astype(jnp.float32) + 0.5) / NSHIFT
        real_part = radius * jnp.cos(angle)
        imag_part = radius * jnp.sin(angle)
        iterate = damping * shifted_inverse(eigvectors, eigvalues, rhs, real_part, imag_part)
        for sweep in range(1, SWEEPS):
            first = iterate[..., :NCOL]
            second = iterate[..., NCOL:]
            shifted = jnp.concatenate([real_part * first - imag_part * second, imag_part * first + real_part * second], axis=-1)
            resid = rhs - shifted + operate(iterate)
            iterate = iterate + damping * shifted_inverse(eigvectors, eigvalues, resid, real_part, imag_part)
        term = real_part / NSHIFT * iterate[..., :NCOL] - imag_part / NSHIFT * iterate[..., NCOL:]
        return (total + term, None)
    start = jnp.zeros((NBLK, BLK, NCOL), jnp.float32)
    summed, _ = lax.scan(contour_term, start, jnp.arange(NSHIFT, dtype=jnp.int32))
    field = summed.reshape(NROWS, NCOL)
    gram = jnp.dot(field.T, field, precision=lax.Precision.HIGHEST) / NROWS
    factor = jnp.linalg.cholesky(gram)
    basis = jax.scipy.linalg.solve_triangular(factor, field.T, lower=True).T
    image = operate(basis.reshape(NBLK, BLK, NCOL)).reshape(NROWS, NCOL)
    projected = jnp.dot(basis.T, image, precision=lax.Precision.HIGHEST) / NROWS
    return (basis, image, projected)
```

```python
import functools

import jax
import jax.numpy as jnp
import numpy as np
from jax import lax
from jax.experimental import pallas as pl
from jax.experimental.pallas import tpu as pltpu
from jax.sharding import PartitionSpec as P

RADIUS = 1.0
DAMPING = 0.8
KEEP = 1.0 - DAMPING
CHUNKS = 4
VMEM_LIMIT = 24 * 1024 * 1024
F32 = jnp.float32
BF16 = jnp.bfloat16


def split(value):
    high = value.astype(BF16)
    low = (value - high.astype(F32)).astype(BF16)
    return high, low


def dot(left, right):
    return jnp.dot(left, right, preferred_element_type=F32)


def dot_three(stacked, high, low):
    half = stacked.shape[0] // 2
    both = dot(stacked, high)
    return both[:half] + both[half:] + dot(stacked[:half], low)


def apply_three(stacked, value):
    return dot_three(stacked, *split(value))


def exact(left, right, contract):
    return lax.dot_general(
        left, right, (contract, ((), ())), precision=lax.Precision.HIGHEST,
        preferred_element_type=F32,
    )


def lane_group(shape, width):
    return lax.broadcasted_iota(jnp.int32, shape, len(shape) - 1) // width


def spread(value, group, width):
    kept = jnp.where(lane_group(value.shape, width) == group, value, 0.0)
    return fold(kept, width)


def fold(value, width):
    lanes = value.shape[-1]
    groups = lanes // width
    if groups & (groups - 1) == 0:
        step = lanes // 2
        while step >= width:
            value = value + pltpu.roll(value, step, value.ndim - 1)
            step //= 2
        return value
    total = value
    for k in range(1, groups):
        total = total + pltpu.roll(value, k * width, value.ndim - 1)
    return total


def column_of(row):
    n = row.shape[1]
    shape = (n, n)
    diagonal = lax.broadcasted_iota(jnp.int32, shape, 0) == lax.broadcasted_iota(jnp.int32, shape, 1)
    return jnp.sum(jnp.where(diagonal, jnp.broadcast_to(row, shape), 0.0), axis=1, keepdims=True)


def inverse_scale(points, energy):
    offset = points[0:1, :] - energy
    imag = points[1:2, :]
    inverse = 1.0 / (offset * offset + imag * imag)
    return offset * inverse, -(imag * inverse)


def call(kernel, out_shape, grid=None, in_specs=None, out_specs=None, scratch=(), flops=0, bytes_accessed=0):
    extra = {}
    if grid is not None:
        extra["grid"] = grid
    return pl.pallas_call(
        kernel,
        out_shape=out_shape,
        in_specs=in_specs,
        out_specs=out_specs,
        scratch_shapes=list(scratch),
        compiler_params=pltpu.CompilerParams(vmem_limit_bytes=VMEM_LIMIT),
        cost_estimate=pl.CostEstimate(flops=flops, bytes_accessed=bytes_accessed, transcendentals=0),
        **extra,
    )


VMEM = functools.partial(pl.BlockSpec, memory_space=pltpu.VMEM)
SMEM = functools.partial(pl.BlockSpec, memory_space=pltpu.SMEM)


def whole(shape):
    return pl.BlockSpec(shape, lambda i: (0,) * len(shape))


def per_device(neighbours, couplings, eigvectors, eigvalues, start_block):
    blk_dev, blk = eigvalues.shape
    nnb = neighbours.shape[1]
    ncol = start_block.shape[1]
    rows_here = blk_dev * blk
    count = lax.axis_size("shift")
    nrows = lax.axis_size("rows")
    total = rows_here * nrows
    width = ncol // count
    packs = blk_dev // count
    wide = 2 * ncol
    here = lax.axis_index("shift")
    me = lax.axis_index("rows")
    paired = nrows % 2 == 0
    halves = 2 if count % 2 == 0 else 1
    per_half = blk_dev // halves
    half_id = here % halves

    angle = np.pi * (np.arange(count, dtype=np.float64) + 0.5) / count
    table = np.zeros((8, ncol), np.float32)
    table[0] = np.repeat(RADIUS * np.cos(angle), width)
    table[1] = np.repeat(RADIUS * np.sin(angle), width)
    table[2] = table[0] / count
    table[3] = table[1] / count
    points = jnp.asarray(table)

    def swap(value):
        if paired:
            return lax.ppermute(value, "rows", [(i, i ^ 1) for i in range(nrows)])
        return lax.ppermute(value, "rows", [(i + 1, i) for i in range(nrows - 1)])

    def pass_on(value, arrived):
        if paired:
            pairs = [(i, i + 2) for i in range(0, nrows - 2, 2)] + [(i, i - 2) for i in range(3, nrows, 2)]
            return lax.ppermute(arrived, "rows", pairs)
        return lax.ppermute(value, "rows", [(i, i + 1) for i in range(nrows - 1)])

    def halo(values):
        first = [swap(v) for v in values]
        second = [pass_on(v, a) for v, a in zip(values, first)]
        return first, second

    def mate(value):
        return lax.ppermute(value, "shift", [(i, i ^ 1) for i in range(count)])

    def gather_shift(value):
        return lax.all_gather(value, "shift")

    def sum_rows(value):
        if nrows & (nrows - 1):
            return lax.psum(value, "rows")
        step = 1
        while step < nrows:
            value = value + lax.ppermute(value, "rows", [(i, i ^ step) for i in range(nrows)])
            step *= 2
        return value

    place = neighbours - (me * blk_dev - blk_dev)
    group = place // blk_dev
    partner_group = jnp.where(me % 2 == 0, 2, 0) if paired else 2
    slot = place % blk_dev + blk_dev * jnp.where(group == 1, 0, jnp.where(group == partner_group, 1, 2))
    slot = slot.astype(jnp.int32)
    position = jnp.stack([here, half_id]).astype(jnp.int32)

    mine = lax.dynamic_slice_in_dim(eigvectors, half_id * per_half, per_half, axis=0)
    cuts = 2 if per_half % 2 == 0 else 1
    sends = jnp.split(mine, cuts, axis=0)
    vec_first, vec_second = halo(sends)
    if halves == 2:
        mate_first = [mate(v) for v in vec_first]
        mate_second = [mate(v) for v in vec_second]
    else:
        mate_first, mate_second = [], []

    def prepare(pos, pts, start, vec, val, spun, packed, vec_st, vec_ts, scale):
        pts = pts[...]
        for i in range(blk_dev):
            tiled = spread(start[i * blk:(i + 1) * blk, :], pos[0], width)
            v = vec[i]
            vh, vl = split(v)
            vec_st[i, :blk, :] = vh
            vec_st[i, blk:, :] = vl
            th, tl = split(v.T)
            vec_ts[i, :blk, :] = th
            vec_ts[i, blk:, :] = tl
            turned = dot_three(jnp.concatenate([th, tl], axis=0), *split(tiled))
            spun[i] = turned
            rows = slice((i // count) * blk, (i // count + 1) * blk)
            kept = jnp.where(lane_group(turned.shape, width) == i % count, turned, 0.0)
            if i % count == 0:
                packed[rows, :] = kept
            else:
                packed[rows, :] += kept
            re, im = inverse_scale(pts, column_of(val[i:i + 1, :]))
            scale[i, :, :ncol] = re
            scale[i, :, ncol:] = im
        packed[packs * blk:, :] = val[...]

    sds = jax.ShapeDtypeStruct
    spun, packed, vec_st, vec_ts, scale = call(
        prepare,
        (
            sds((blk_dev, blk, ncol), F32),
            sds((packs * blk + blk_dev, ncol), F32),
            sds((blk_dev, 2 * blk, blk), BF16),
            sds((blk_dev, 2 * blk, blk), BF16),
            sds((blk_dev, blk, wide), F32),
        ),
        in_specs=[SMEM(), VMEM(), VMEM(), VMEM(), VMEM()],
        out_specs=[VMEM()] * 5,
        flops=6 * blk_dev * blk * blk * ncol,
        bytes_accessed=4 * 6 * blk_dev * blk * blk,
    )(position, points, start_block, eigvectors, eigvalues)

    (pack_first,), (pack_second,) = halo([packed])

    def couple(coup, spun_ref, scale_ref, vec, cst, xh, xl):
        for k in range(nnb):
            ch, cl = split(coup[0, k])
            cst[0, :blk, k * blk:(k + 1) * blk] = ch
            cst[0, blk:, k * blk:(k + 1) * blk] = cl
        b = DAMPING * spun_ref[0]
        s = scale_ref[0]
        x = apply_three(vec[0], jnp.concatenate([s[:, :ncol] * b, s[:, ncol:] * b], axis=1))
        h, l = split(x)
        xh[...] = h
        xl[...] = l

    def block_of(*shape):
        return pl.BlockSpec((1,) + shape, lambda i: (i,) + (0,) * len(shape))

    cst, own_h, own_l = call(
        couple,
        (
            sds((blk_dev, 2 * blk, nnb * blk), BF16),
            sds((rows_here, wide), BF16),
            sds((rows_here, wide), BF16),
        ),
        grid=(blk_dev,),
        in_specs=[block_of(nnb, blk, blk), block_of(blk, ncol), block_of(blk, wide), block_of(2 * blk, blk)],
        out_specs=[
            block_of(2 * blk, nnb * blk),
            pl.BlockSpec((blk, wide), lambda i: (i, 0)),
            pl.BlockSpec((blk, wide), lambda i: (i, 0)),
        ],
        flops=6 * blk_dev * blk * blk * wide,
        bytes_accessed=8 * blk_dev * nnb * blk * blk,
    )(couplings, spun, scale, vec_st)

    n_vec = halves * cuts

    def first_iterate(*refs):
        pos, pts, oh, ol = refs[:4]
        sides = [refs[4:4 + n_vec], refs[4 + n_vec:4 + 2 * n_vec]]
        packs_in = refs[4 + 2 * n_vec:6 + 2 * n_vec]
        xh, xl = refs[6 + 2 * n_vec:]
        xh[:rows_here, :] = oh[...]
        xl[:rows_here, :] = ol[...]
        pts = pts[...]
        per_cut = per_half // cuts
        for side in range(2):
            pack = packs_in[side]
            for h in range(halves):
                base = ((pos[1] + h) % halves) * per_half if halves > 1 else 0
                for c in range(cuts):
                    for j in range(per_cut):
                        b = base + c * per_cut + j
                        row0 = pl.multiple_of((b // count) * blk, blk)
                        turned = spread(pack[pl.ds(row0, blk), :], b % count, width) * DAMPING
                        re, im = inverse_scale(pts, column_of(pack[pl.ds(packs * blk + b, 1), :]))
                        v = sides[side][h * cuts + c][j]
                        vh, vl = split(v)
                        x = apply_three(
                            jnp.concatenate([vh, vl], axis=0),
                            jnp.concatenate([re * turned, im * turned], axis=1),
                        )
                        out0 = pl.multiple_of((b + blk_dev * (1 + side)) * blk, blk)
                        h1, l1 = split(x)
                        xh[pl.ds(out0, blk), :] = h1
                        xl[pl.ds(out0, blk), :] = l1

    field_shape = (sds((3 * rows_here, wide), BF16), sds((3 * rows_here, wide), BF16))
    vec_in = vec_first + mate_first + vec_second + mate_second
    one_h, one_l = call(
        first_iterate,
        field_shape,
        in_specs=[SMEM()] + [VMEM()] * (5 + len(vec_in)),
        out_specs=[VMEM()] * 2,
        flops=12 * blk_dev * blk * blk * wide,
        bytes_accessed=4 * 6 * blk_dev * blk * blk,
    )(position, points, own_h, own_l, *vec_in, pack_first, pack_second)

    def near_of(ref, slots, i):
        return jnp.concatenate(
            [ref[pl.ds(pl.multiple_of(slots[i, k] * blk, blk), blk), :] for k in range(nnb)], axis=0
        )

    def times(s, g):
        re, im = g[:, :ncol], g[:, ncol:]
        sre, sim = s[:, :ncol], s[:, ncol:]
        return jnp.concatenate([sre * re - sim * im, sre * im + sim * re], axis=1)

    def plus_real(g, b):
        return jnp.concatenate([g[:, :ncol] + b, g[:, ncol:]], axis=1)

    def second_iterate(base, slots, xh, xl, c, vec, vec_t, spun_ref, scale_ref, out, out_hat):
        i = pl.program_id(0) + base
        s = dot_three(c[0], near_of(xh, slots, i), near_of(xl, slots, i))
        g = plus_real(apply_three(vec_t[0], s), (1.0 + KEEP) * spun_ref[0])
        hat = times(scale_ref[0], DAMPING * g)
        out_hat[0] = hat
        out[0] = apply_three(vec[0], hat)

    chunks = CHUNKS if blk_dev % CHUNKS == 0 else 1
    per_chunk = blk_dev // chunks

    def shifted(base, *shape):
        return pl.BlockSpec((1,) + shape, lambda i: (i + base,) + (0,) * len(shape))

    own, own_hat = [], []
    for c in range(chunks):
        base = c * per_chunk
        out, hat = call(
            functools.partial(second_iterate, base),
            (sds((per_chunk, blk, wide), F32), sds((per_chunk, blk, wide), F32)),
            grid=(per_chunk,),
            in_specs=[
                SMEM(), whole((3 * rows_here, wide)), whole((3 * rows_here, wide)),
                shifted(base, 2 * blk, nnb * blk), shifted(base, 2 * blk, blk), shifted(base, 2 * blk, blk),
                shifted(base, blk, ncol), shifted(base, blk, wide),
            ],
            out_specs=[block_of(blk, wide), block_of(blk, wide)],
            flops=6 * per_chunk * (nnb + 2) * blk * blk * wide,
            bytes_accessed=4 * 3 * rows_here * wide + 4 * per_chunk * nnb * blk * blk,
        )(slot, one_h, one_l, cst, vec_st, vec_ts, spun, scale)
        own.append(out)
        own_hat.append(hat)

    two_first, two_second = halo(own)

    def third_iterate(*refs):
        slots, pts = refs[:2]
        fields = refs[2:2 + 3 * chunks]
        hats = refs[2 + 3 * chunks:2 + 4 * chunks]
        c, vec, vec_t, spun_ref, scale_ref, val = refs[2 + 4 * chunks:8 + 4 * chunks]
        packed_out, diag_out, xh, xl = refs[8 + 4 * chunks:]
        i = pl.program_id(0)

        @pl.when(i == 0)
        def _():
            for f, field in enumerate(fields):
                for j in range(per_chunk):
                    rows = slice((f * per_chunk + j) * blk, (f * per_chunk + j + 1) * blk)
                    h, l = split(field[j])
                    xh[rows, :] = h
                    xl[rows, :] = l
            packed_out[...] = jnp.zeros_like(packed_out)

        s = dot_three(c[0], near_of(xh, slots, i), near_of(xl, slots, i))
        g = plus_real(apply_three(vec_t[0], s), spun_ref[0])
        hat = hats[0][i % per_chunk]
        for q in range(1, chunks):
            hat = jnp.where(i // per_chunk == q, hats[q][i % per_chunk], hat)
        hat = KEEP * hat + times(scale_ref[0], DAMPING * g)
        term = pts[2:3, :] * hat[:, :ncol] - pts[3:4, :] * hat[:, ncol:]
        turned = fold(term, width)
        energy = column_of(val[pl.ds(i, 1), :])
        both = apply_three(vec[0], jnp.concatenate([turned, energy * turned], axis=1))
        diag_out[0] = both[:, ncol:]
        rows = pl.ds(pl.multiple_of((i // count) * blk, blk), blk)
        packed_out[rows, :] += jnp.where(
            lane_group((blk, ncol), width) == i % count, both[:, :ncol], 0.0
        )

    chunk_spec = whole((per_chunk, blk, wide))
    filtered, diagonal = call(
        third_iterate,
        (sds((packs * blk, ncol), F32), sds((blk_dev, blk, ncol), F32)),
        grid=(blk_dev,),
        in_specs=[SMEM(), whole(points.shape)] + [chunk_spec] * (4 * chunks) + [
            block_of(2 * blk, nnb * blk), block_of(2 * blk, blk), block_of(2 * blk, blk),
            block_of(blk, ncol), block_of(blk, wide), whole((blk_dev, blk)),
        ],
        out_specs=[whole((packs * blk, ncol)), block_of(blk, ncol)],
        scratch=[pltpu.VMEM((3 * rows_here, wide), BF16)] * 2,
        flops=6 * blk_dev * (nnb + 2) * blk * blk * wide,
        bytes_accessed=4 * 4 * rows_here * wide + 4 * blk_dev * nnb * blk * blk,
    )(slot, points, *own, *two_first, *two_second, *own_hat, cst, vec_st, vec_ts, spun, scale, eigvalues)

    (filt_first,), (filt_second,) = halo([filtered])
    filt_all = gather_shift(filtered)

    def unpacked(ref, i):
        rows = slice((i // count) * blk, (i // count + 1) * blk)
        lanes = lane_group((blk, ncol), width)
        out = jnp.zeros((blk, ncol), F32)
        for s in range(count):
            moved = ref[s, rows, :]
            turn = ((s - i % count) * width) % ncol
            if turn:
                moved = pltpu.roll(moved, turn, 1)
            out = jnp.where(lanes == s, moved, out)
        return out

    def gram_of(pieces, full, gram):
        acc = jnp.zeros((ncol, ncol), F32)
        for i in range(blk_dev):
            f = unpacked(pieces, i)
            full[i * blk:(i + 1) * blk, :] = f
            acc = acc + exact(f, f, ((0,), (0,)))
        gram[...] = acc

    full, gram = call(
        gram_of,
        (sds((rows_here, ncol), F32), sds((ncol, ncol), F32)),
        in_specs=[VMEM()], out_specs=[VMEM()] * 2,
        flops=12 * rows_here * ncol * ncol, bytes_accessed=8 * rows_here * ncol,
    )(filt_all)
    gram = sum_rows(gram)

    def image_of(slots, own_f, first_f, second_f, full_ref, c, diag, packed_out, moment, xh, xl):
        i = pl.program_id(0)

        @pl.when(i == 0)
        def _():
            for f, field in enumerate((own_f, first_f, second_f)):
                for b in range(blk_dev):
                    piece = field[(b // count) * blk:(b // count + 1) * blk, :]
                    h, l = split(spread(piece, b % count, width))
                    rows = slice((f * blk_dev + b) * blk, (f * blk_dev + b + 1) * blk)
                    xh[rows, :] = h
                    xl[rows, :] = l
            packed_out[...] = jnp.zeros_like(packed_out)
            moment[...] = jnp.zeros_like(moment)

        image = diag[0] + dot_three(c[0], near_of(xh, slots, i), near_of(xl, slots, i))
        rows = pl.ds(pl.multiple_of((i // count) * blk, blk), blk)
        lanes = lane_group((blk, ncol), width)
        packed_out[rows, :] += jnp.where(lanes == i % count, image, 0.0)
        part = exact(full_ref[...], image, ((0,), (0,)))
        span = ncol // count
        piece = jnp.zeros((span, ncol), F32)
        for s in range(count):
            piece = piece + jnp.where(
                lane_group((span, ncol), width) == s, part[s * span:(s + 1) * span, :], 0.0
            )
        moment[...] += piece

    image, moment = call(
        image_of,
        (sds((packs * blk, ncol), F32), sds((ncol // count, ncol), F32)),
        grid=(blk_dev,),
        in_specs=[SMEM()] + [whole((packs * blk, ncol))] * 3 + [
            pl.BlockSpec((blk, ncol), lambda i: (i, 0)),
            block_of(2 * blk, nnb * blk), block_of(blk, ncol),
        ],
        out_specs=[whole((packs * blk, ncol)), whole((ncol // count, ncol))],
        scratch=[pltpu.VMEM((3 * rows_here, ncol), BF16)] * 2,
        flops=6 * blk_dev * (nnb + 2) * blk * blk * ncol,
        bytes_accessed=4 * blk_dev * nnb * blk * blk,
    )(slot, filtered, filt_first, filt_second, full, cst, diagonal)

    image_all = gather_shift(image)
    moment_all = gather_shift(sum_rows(moment))

    def factor_of(gram_ref, full_ref, inverse, basis_ref):
        tiles = ncol // 8
        a = [gram_ref[t * 8:(t + 1) * 8, :] * (1.0 / total) for t in range(tiles)]
        lanes = lax.broadcasted_iota(jnp.int32, (8, ncol), 1)
        subs = lax.broadcasted_iota(jnp.int32, (8, ncol), 0)
        e = [jnp.where(lanes == subs + t * 8, 1.0, 0.0).astype(F32) for t in range(tiles)]
        for k in range(ncol):
            t, q = divmod(k, 8)
            rp = 1.0 / a[t][q:q + 1, k:k + 1]
            row = a[t][q:q + 1, :] * rp
            erow = e[t][q:q + 1, :] * rp
            for u in range(t, tiles):
                m = jnp.broadcast_to(a[u][:, k:k + 1], (8, ncol))
                if u == t:
                    m = jnp.where(subs > q, m, 0.0)
                a[u] = a[u] - m * row
                e[u] = e[u] - m * erow
        for t in range(tiles):
            pivot = jnp.sum(jnp.where(lanes == subs + t * 8, a[t], 0.0), axis=1, keepdims=True)
            inverse[t * 8:(t + 1) * 8, :] = e[t] * (1.0 / jnp.sqrt(pivot))
        basis_ref[...] = exact(full_ref[...], inverse[...], ((1,), (1,)))

    inverse, basis = call(
        factor_of,
        (sds((ncol, ncol), F32), sds((rows_here, ncol), F32)),
        in_specs=[VMEM()] * 2, out_specs=[VMEM()] * 2,
        flops=12 * rows_here * ncol * ncol, bytes_accessed=8 * rows_here * ncol,
    )(gram, full)

    def project(pieces, moments, inv_ref, image_ref, projected_ref):
        inv = inv_ref[...]
        for i in range(blk_dev):
            image_ref[i * blk:(i + 1) * blk, :] = exact(unpacked(pieces, i), inv, ((1,), (1,)))
        span = ncol // count
        lanes = lane_group((span, ncol), width)
        strips = []
        for g in range(count):
            out = jnp.zeros((span, ncol), F32)
            for s in range(count):
                moved = moments[s]
                turn = ((s - g) * width) % ncol
                if turn:
                    moved = pltpu.roll(moved, turn, 1)
                out = jnp.where(lanes == s, moved, out)
            strips.append(out)
        m = jnp.concatenate(strips, axis=0) * (1.0 / total)
        projected_ref[...] = exact(exact(inv, m, ((1,), (0,))), inv, ((1,), (1,)))

    basis_image, projected = call(
        project,
        (sds((rows_here, ncol), F32), sds((ncol, ncol), F32)),
        in_specs=[VMEM()] * 3, out_specs=[VMEM()] * 2,
        flops=12 * rows_here * ncol * ncol, bytes_accessed=8 * rows_here * ncol,
    )(image_all, moment_all, inverse)
    return (basis, basis_image, projected)


def solution(mesh):
    in_specs = (
        P("rows", None),
        P("rows", None, None, None),
        P("rows", None, None),
        P("rows", None),
        P("rows", None),
    )
    out_specs = (P("rows", None), P("rows", None), P())
    return jax.shard_map(
        per_device, mesh=mesh, in_specs=in_specs, out_specs=out_specs, check_vma=False
    )
```

```python
import functools

import jax
import jax.numpy as jnp
import numpy as np
from jax import lax
from jax.experimental import pallas as pl
from jax.experimental.pallas import tpu as pltpu
from jax.sharding import PartitionSpec as P

RADIUS = 1.0
DAMPING = 0.8
CHUNKS = 4
KEEP = 1.0 - DAMPING
VMEM_LIMIT = 24 * 1024 * 1024
FLOPS_PER_MICRO = 1.1e9
GRAM_MICROS = 6.0
F32 = jnp.float32
BF16 = jnp.bfloat16


def split(value):
    high = value.astype(BF16)
    low = (value - high.astype(F32)).astype(BF16)
    return high, low


def dot(left, right):
    return jnp.dot(left, right, preferred_element_type=F32)


def dot_three(stacked, high, low):
    half = stacked.shape[0] // 2
    both = dot(stacked, high)
    return both[:half] + both[half:] + dot(stacked[:half], low)


def apply_three(stacked, value):
    return dot_three(stacked, *split(value))


def exact(left, right, contract):
    return lax.dot_general(
        left, right, (contract, ((), ())), precision=lax.Precision.HIGHEST,
        preferred_element_type=F32,
    )


def lane_group(shape, width):
    return lax.broadcasted_iota(jnp.int32, shape, len(shape) - 1) // width


def spread(value, group, width):
    kept = jnp.where(lane_group(value.shape, width) == group, value, 0.0)
    return fold(kept, width)


def fold(value, width):
    lanes = value.shape[-1]
    groups = lanes // width
    if groups & (groups - 1) == 0:
        step = lanes // 2
        while step >= width:
            value = value + pltpu.roll(value, step, value.ndim - 1)
            step //= 2
        return value
    total = value
    for k in range(1, groups):
        total = total + pltpu.roll(value, k * width, value.ndim - 1)
    return total


def column_of(row):
    n = row.shape[1]
    shape = (n, n)
    diagonal = lax.broadcasted_iota(jnp.int32, shape, 0) == lax.broadcasted_iota(jnp.int32, shape, 1)
    return jnp.sum(jnp.where(diagonal, jnp.broadcast_to(row, shape), 0.0), axis=1, keepdims=True)


def lane_table(values, shape, width):
    groups = lane_group(shape, width)
    out = jnp.full(shape, float(values[0]), F32)
    for j in range(1, len(values)):
        out = jnp.where(groups == j, float(values[j]), out)
    return out


def call(kernel, out_shape, in_specs, scratch=(), micros=1.0):
    single = not isinstance(out_shape, (tuple, list))
    return pl.pallas_call(
        kernel,
        out_shape=out_shape,
        in_specs=in_specs,
        out_specs=VMEM() if single else [VMEM()] * len(out_shape),
        scratch_shapes=list(scratch),
        compiler_params=pltpu.CompilerParams(vmem_limit_bytes=VMEM_LIMIT),
        cost_estimate=pl.CostEstimate(flops=int(micros * FLOPS_PER_MICRO), bytes_accessed=0, transcendentals=0),
    )


VMEM = functools.partial(pl.BlockSpec, memory_space=pltpu.VMEM)
SMEM = functools.partial(pl.BlockSpec, memory_space=pltpu.SMEM)
HBM = functools.partial(pl.BlockSpec, memory_space=pltpu.HBM)


def per_device(neighbours, couplings, eigvectors, eigvalues, start_block):
    blk_dev, blk = eigvalues.shape
    nnb = neighbours.shape[1]
    ncol = start_block.shape[1]
    rows_here = blk_dev * blk
    count = lax.axis_size("shift")
    nrows = lax.axis_size("rows")
    total = rows_here * nrows
    width = ncol // count
    packs = blk_dev // count
    wide = 2 * ncol
    here = lax.axis_index("shift")
    me = lax.axis_index("rows")
    paired = nrows % 2 == 0
    halves = 2 if count % 2 == 0 else 1
    per_half = blk_dev // halves
    half_id = here % halves

    angle = np.pi * (np.arange(count, dtype=np.float64) + 0.5) / count
    real_parts = RADIUS * np.cos(angle)
    imag_parts = RADIUS * np.sin(angle)

    def inverse_scale(energy):
        offset = lane_table(real_parts, (1, ncol), width) - energy
        imag = lane_table(imag_parts, (1, ncol), width)
        inverse = 1.0 / (offset * offset + imag * imag)
        return offset * inverse, -(imag * inverse)

    def own_group():
        return lax.axis_index("shift")

    def block_rows(i):
        return slice((i // count) * blk, (i // count + 1) * blk)

    def store_packed(ref, i, value):
        kept = jnp.where(lane_group(value.shape, width) == i % count, value, 0.0)
        if i % count == 0:
            ref[block_rows(i), :] = kept
        else:
            ref[block_rows(i), :] += kept

    def swap(value):
        if paired:
            return lax.ppermute(value, "rows", [(i, i ^ 1) for i in range(nrows)])
        return lax.ppermute(value, "rows", [(i + 1, i) for i in range(nrows - 1)])

    def pass_on(value, arrived):
        if paired:
            pairs = [(i, i + 2) for i in range(0, nrows - 2, 2)] + [(i, i - 2) for i in range(3, nrows, 2)]
            return lax.ppermute(arrived, "rows", pairs)
        return lax.ppermute(value, "rows", [(i, i + 1) for i in range(nrows - 1)])

    def after(value, *others):
        return lax.optimization_barrier((value,) + others)[0]

    def halo(values):
        first = [swap(v) for v in values]
        second = [pass_on(v, a) for v, a in zip(values, first)]
        return first, second

    def mate(value):
        return lax.ppermute(value, "shift", [(i, i ^ 1) for i in range(count)])

    def gather_pairs(value):
        if count & (count - 1):
            return gather_shift(value)
        rows_each = value.shape[0]
        step = 1
        while step < count:
            value = jnp.concatenate(
                [value, lax.ppermute(value, "shift", [(i, i ^ step) for i in range(count)])], axis=0
            )
            step *= 2
        return [value[k * rows_each:(k + 1) * rows_each] for k in range(count)]

    def gather_shift(value):
        return [value] + [
            lax.ppermute(value, "shift", [(source(i, k), i) for i in range(count)]) for k in range(1, count)
        ]

    def source(i, k):
        return i ^ k if count & (count - 1) == 0 else (i + count - k) % count

    def sum_rows(value):
        if nrows & (nrows - 1):
            return lax.psum(value, "rows")
        step = 1
        while step < nrows:
            value = value + lax.ppermute(value, "rows", [(i, i ^ step) for i in range(nrows)])
            step *= 2
        return value

    place = neighbours - (me * blk_dev - blk_dev)
    group = place // blk_dev
    partner_group = jnp.where(me % 2 == 0, 2, 0) if paired else 2
    slot = place % blk_dev + blk_dev * jnp.where(group == 1, 0, jnp.where(group == partner_group, 1, 2))
    slot = slot.astype(jnp.int32)

    mine = lax.dynamic_slice_in_dim(eigvectors, half_id * per_half, per_half, axis=0)
    cuts = 1
    per_cut = per_half // cuts
    sends = [v.reshape(per_cut * blk, blk) for v in jnp.split(mine, cuts, axis=0)]
    sends[0] = jnp.concatenate([sends[0], eigvalues], axis=0)
    vec_first = [swap(v) for v in sends]
    def prepare(start_hbm, vec_hbm, spun, packed, vec_st, vec_ts, start, vec, sems):
        copies = []
        for i in range(blk_dev):
            rows = pl.ds(i * blk, blk)
            copies.append(pltpu.make_async_copy(vec_hbm.at[i], vec.at[i], sems.at[i]))
            copies.append(pltpu.make_async_copy(start_hbm.at[rows], start.at[rows], sems.at[blk_dev + i]))
        for copy in copies:
            copy.start()
        for copy in copies:
            copy.wait()
        mine_now = own_group()
        lefts, rights = [], []
        for i in range(blk_dev):
            v = vec[i]
            vh, vl = split(v)
            vec_st[i, :blk, :] = vh
            vec_st[i, blk:, :] = vl
            th, tl = split(v.T)
            vec_ts[i, :blk, :] = th
            vec_ts[i, blk:, :] = tl
            lefts.append(jnp.concatenate([th, tl], axis=0))
            rights.append(split(spread(start[i * blk:(i + 1) * blk, :], mine_now, width)))
        turned = [dot_three(left, *right) for left, right in zip(lefts, rights)]
        for i in range(blk_dev):
            spun[i] = turned[i]
            store_packed(packed, i, turned[i])

    sds = jax.ShapeDtypeStruct
    spun, packed, vec_st, vec_ts = call(
        prepare,
        (
            sds((blk_dev, blk, ncol), F32),
            sds((packs * blk, ncol), F32),
            sds((blk_dev, 2 * blk, blk), BF16),
            sds((blk_dev, 2 * blk, blk), BF16),
        ),
        in_specs=[HBM()] * 2,
        scratch=[
            pltpu.VMEM((rows_here, ncol), F32), pltpu.VMEM((blk_dev, blk, blk), F32),
            pltpu.SemaphoreType.DMA((2 * blk_dev,)),
        ],
        micros=2.5,
    )(start_block, eigvectors)

    vec_first = [after(v, packed) for v in vec_first]
    vec_second = [pass_on(v, a) for v, a in zip(sends, vec_first)]
    mate_first = [mate(v[:per_cut * blk]) for v in vec_first] if halves == 2 else []
    pack_first = swap(packed)
    pack_second = pass_on(packed, after(pack_first, *mate_first))
    begun = (pack_first, *mate_first)

    def couple(coup_hbm, spun_ref, val, vec, cst, xh, xl, scale_ref, coup, sems):
        copies = [pltpu.make_async_copy(coup_hbm.at[i], coup.at[i], sems.at[i]) for i in range(blk_dev)]
        for copy in copies:
            copy.start()
        fields = []
        for i in range(blk_dev):
            b = DAMPING * spun_ref[i]
            re, im = inverse_scale(column_of(val[i:i + 1, :]))
            scale_ref[i, :, :ncol] = re
            scale_ref[i, :, ncol:] = im
            fields.append(apply_three(vec[i], jnp.concatenate([re * b, im * b], axis=1)))
        for i in range(blk_dev):
            put(xh, xl, i, fields[i])
        for i in range(blk_dev):
            copies[i].wait()
            for k in range(nnb):
                ch, cl = split(coup[i, k])
                cst[i, :blk, k * blk:(k + 1) * blk] = ch
                cst[i, blk:, k * blk:(k + 1) * blk] = cl

    def put(xh, xl, block, value):
        rows = pl.ds(pl.multiple_of(block * blk, blk), blk)
        h, l = split(value)
        xh[rows, :] = h
        xl[rows, :] = l

    field_shape = (sds((rows_here, wide), BF16), sds((rows_here, wide), BF16))
    cst, own_h, own_l, scale = call(
        couple,
        (sds((blk_dev, 2 * blk, nnb * blk), BF16),) + field_shape + (sds((blk_dev, blk, wide), F32),),
        in_specs=[HBM()] + [VMEM()] * 3,
        scratch=[pltpu.VMEM((blk_dev, nnb, blk, blk), F32), pltpu.SemaphoreType.DMA((blk_dev,))],
        micros=2.5,
    )(after(couplings, *begun), spun, eigvalues, vec_st)

    vec_second = [after(v, cst) for v in vec_second]
    mate_second = [mate(v[:per_cut * blk]) for v in vec_second] if halves == 2 else []

    def fill_first(inputs, xh, xl, offset):
        pack = inputs[0]
        vecs = inputs[1:]
        names, lefts, rights = [], [], []
        for h in range(halves):
            base = ((lax.axis_index("shift") + h) % halves) * per_half if halves > 1 else 0
            for c in range(cuts):
                for j in range(per_cut):
                    b = base + c * per_cut + j
                    row0 = pl.multiple_of((b // count) * blk, blk)
                    turned = spread(pack[pl.ds(row0, blk), :], b % count, width) * DAMPING
                    re, im = inverse_scale(column_of(vecs[0][pl.ds(per_cut * blk + b, 1), :]))
                    names.append(b)
                    lefts.append(jnp.concatenate(split(vecs[h * cuts + c][j * blk:(j + 1) * blk, :]), axis=0))
                    rights.append(jnp.concatenate([re * turned, im * turned], axis=1))
        fields = [apply_three(left, right) for left, right in zip(lefts, rights)]
        for b, field in zip(names, fields):
            put(xh, xl, b + offset, field)

    def first_partner(*refs):
        fill_first(refs[:-2], refs[-2], refs[-1], 0)

    partners = [pack_first] + vec_first + mate_first
    partner_h, partner_l = call(
        first_partner,
        field_shape,
        in_specs=[VMEM()] * len(partners),
        micros=1.5,
    )(*partners)

    def near_of(ref, slots, i):
        return jnp.concatenate(
            [ref[pl.ds(pl.multiple_of(slots[i, k] * blk, blk), blk), :] for k in range(nnb)], axis=0
        )

    def coupled(slots, c, xh, xl, i):
        return dot_three(c[i], near_of(xh, slots, i), near_of(xl, slots, i))

    def times(s, g):
        re, im = g[:, :ncol], g[:, ncol:]
        sre, sim = s[:, :ncol], s[:, ncol:]
        return jnp.concatenate([sre * re - sim * im, sre * im + sim * re], axis=1)

    def plus_real(g, b):
        return jnp.concatenate([g[:, :ncol] + b, g[:, ncol:]], axis=1)

    sizes = [blk_dev // CHUNKS] * CHUNKS if blk_dev % CHUNKS == 0 else [blk_dev]
    chunks = len(sizes)
    spots = [(c, j) for c in range(chunks) for j in range(sizes[c])]

    others = [pack_second] + vec_second + mate_second

    def second_iterate(*refs):
        slots, oh, ol, ph, pl_, c, vec, vec_t, spun_ref, scale_ref = refs[:10]
        inputs = refs[10:10 + len(others)]
        outs = refs[10 + len(others):10 + len(others) + chunks]
        hats, xh, xl = refs[10 + len(others) + chunks:]
        fill_first(inputs, xh, xl, 2 * blk_dev)
        xh[:rows_here, :] = oh[...]
        xl[:rows_here, :] = ol[...]
        xh[rows_here:2 * rows_here, :] = ph[...]
        xl[rows_here:2 * rows_here, :] = pl_[...]
        blocks = range(blk_dev)
        sums = [coupled(slots, c, xh, xl, i) for i in blocks]
        turned = [apply_three(vec_t[i], sums[i]) for i in blocks]
        for i in blocks:
            hats[i] = times(scale_ref[i], DAMPING * plus_real(turned[i], (1.0 + KEEP) * spun_ref[i]))
        result = [apply_three(vec[i], hats[i]) for i in blocks]
        for i in blocks:
            q, j = spots[i]
            outs[q][j] = result[i]

    field_scratch = [pltpu.VMEM((3 * rows_here, wide), BF16)] * 2
    *own, hats = call(
        second_iterate,
        [sds((size, blk, wide), F32) for size in sizes] + [sds((blk_dev, blk, wide), F32)],
        in_specs=[SMEM()] + [VMEM()] * (9 + len(others)),
        scratch=field_scratch,
        micros=6.0,
    )(slot, own_h, own_l, partner_h, partner_l, cst, vec_st, vec_ts, spun, scale, *others)

    two_first, two_second = halo(own)

    def third_iterate(*refs):
        slots = refs[0]
        fields = refs[1:1 + 3 * chunks]
        hats_ref, c, vec, vec_t, spun_ref, scale_ref, val = refs[1 + 3 * chunks:8 + 3 * chunks]
        packed_out, diag_out, xh, xl = refs[8 + 3 * chunks:]
        for side in range(3):
            for i, (q, j) in enumerate(spots):
                put(xh, xl, side * blk_dev + i, fields[side * chunks + q][j])
        weight_re = lane_table(real_parts / count, (1, ncol), width)
        weight_im = lane_table(imag_parts / count, (1, ncol), width)
        blocks = range(blk_dev)
        sums = [coupled(slots, c, xh, xl, i) for i in blocks]
        turned = [apply_three(vec_t[i], sums[i]) for i in blocks]
        ends = []
        for i in blocks:
            hat = KEEP * hats_ref[i] + times(scale_ref[i], DAMPING * plus_real(turned[i], spun_ref[i]))
            term = fold(weight_re * hat[:, :ncol] - weight_im * hat[:, ncol:], width)
            energy = column_of(val[i:i + 1, :])
            ends.append(jnp.concatenate([term, energy * term], axis=1))
        result = [apply_three(vec[i], ends[i]) for i in blocks]
        for i in blocks:
            diag_out[i] = result[i][:, ncol:]
            store_packed(packed_out, i, result[i][:, :ncol])

    filtered, diagonal = call(
        third_iterate,
        (sds((packs * blk, ncol), F32), sds((blk_dev, blk, ncol), F32)),
        in_specs=[SMEM()] + [VMEM()] * (7 + 3 * chunks),
        scratch=field_scratch,
        micros=6.0,
    )(slot, *own, *two_first, *two_second, hats, cst, vec_st, vec_ts, spun, scale, eigvalues)

    (filt_first,), (filt_second,) = halo([filtered])
    filt_all = gather_shift(filtered)

    def unpacked(refs, rows, g):
        lanes = lane_group((rows.stop - rows.start, ncol), width)
        out = jnp.zeros(lanes.shape, F32)
        mine_now = own_group()
        for k, ref in enumerate(refs):
            s = source(mine_now, k) if k else mine_now
            moved = pltpu.roll(ref[rows, :], ((s - g + count) % count) * width, 1)
            out = jnp.where(lanes == s, moved, out)
        return out

    def gram_of(*refs):
        pieces, full, gram = refs[:count], refs[count], refs[1 + count]
        for i in range(blk_dev):
            full[i * blk:(i + 1) * blk, :] = unpacked(pieces, block_rows(i), i % count)
        gram[...] = exact(full[...], full[...], ((0,), (0,)))

    full, gram = call(
        gram_of,
        (sds((rows_here, ncol), F32), sds((ncol, ncol), F32)),
        in_specs=[VMEM()] * count,
        micros=GRAM_MICROS,
    )(*filt_all)

    span = ncol // count

    def image_of(slots, own_f, first_f, second_f, full_ref, gram_ref, c, diag, packed_out, sums, xh, xl, image_ref):
        for f, field in enumerate((own_f, first_f, second_f)):
            for b in range(blk_dev):
                put(xh, xl, f * blk_dev + b, spread(field[block_rows(b), :], b % count, width))
        for i in range(blk_dev):
            image = diag[i] + coupled(slots, c, xh, xl, i)
            image_ref[i * blk:(i + 1) * blk, :] = image
            store_packed(packed_out, i, image)
        part = exact(full_ref[...], image_ref[...], ((0,), (0,)))
        piece = jnp.zeros((span, ncol), F32)
        for s in range(count):
            piece = piece + jnp.where(
                lane_group((span, ncol), width) == s, part[s * span:(s + 1) * span, :], 0.0
            )
        sums[:ncol, :] = gram_ref[...]
        sums[ncol:, :] = piece

    image, sums = call(
        image_of,
        (sds((packs * blk, ncol), F32), sds((ncol + span, ncol), F32)),
        in_specs=[SMEM()] + [VMEM()] * 7,
        scratch=[pltpu.VMEM((3 * rows_here, ncol), BF16)] * 2 + [pltpu.VMEM((rows_here, ncol), F32)],
        micros=3.8,
    )(slot, filtered, filt_first, filt_second, full, gram, cst, diagonal)

    image_all = gather_pairs(image)
    sums = sum_rows(sums)
    moment_all = gather_pairs(sums[ncol:])

    def factor_of(sums_ref, inverse):
        tiles = ncol // 8
        a = [sums_ref[t * 8:(t + 1) * 8, :] * (1.0 / total) for t in range(tiles)]
        lanes = lax.broadcasted_iota(jnp.int32, (8, ncol), 1)
        subs = lax.broadcasted_iota(jnp.int32, (8, ncol), 0)
        e = [jnp.where(lanes == subs + t * 8, 1.0, 0.0).astype(F32) for t in range(tiles)]
        for t in range(tiles):
            below = range(t, tiles)
            cols = [
                {u: jnp.broadcast_to(a[u][:, t * 8 + j:t * 8 + j + 1], (8, ncol)) for u in below} for j in range(8)
            ]
            rows = [a[t][j:j + 1, :] for j in range(8)]
            erows = [e[t][j:j + 1, :] for j in range(8)]
            factors = []
            for j in range(8):
                inv = 1.0 / cols[j][t][j:j + 1, :]
                m = {u: cols[j][u] * inv for u in below}
                m[t] = jnp.where(subs > j, m[t], 0.0)
                for q in range(j + 1, 8):
                    above = cols[q][t][j:j + 1, :]
                    for u in below:
                        cols[q][u] = cols[q][u] - m[u] * above
                    left = m[t][q:q + 1, :]
                    rows[q] = rows[q] - left * rows[j]
                    erows[q] = erows[q] - left * erows[j]
                factors.append(m)
            for u in below:
                for j in range(8):
                    a[u] = a[u] - factors[j][u] * rows[j]
                    e[u] = e[u] - factors[j][u] * erows[j]
        for t in range(tiles):
            pivot = jnp.sum(jnp.where(lanes == subs + t * 8, a[t], 0.0), axis=1, keepdims=True)
            inverse[t * 8:(t + 1) * 8, :] = e[t] * (1.0 / jnp.sqrt(pivot))

    inverse = call(
        factor_of, sds((ncol, ncol), F32), in_specs=[VMEM()], micros=5.5,
    )(sums)

    def finish(*refs):
        full_ref, pieces, moments, inv_ref = refs[0], refs[1:1 + count], refs[1 + count:1 + 2 * count], refs[1 + 2 * count]
        basis_ref, image_ref, projected_ref, raw = refs[2 + 2 * count:]
        inv = inv_ref[...]
        strips = [unpacked(moments, slice(0, span), g) for g in range(count)]
        m = jnp.concatenate(strips, axis=0) * (1.0 / total)
        for i in range(blk_dev):
            raw[i * blk:(i + 1) * blk, :] = unpacked(pieces, block_rows(i), i % count)
        half = exact(inv, m, ((1,), (0,)))
        basis_ref[...] = exact(full_ref[...], inv, ((1,), (1,)))
        image_ref[...] = exact(raw[...], inv, ((1,), (1,)))
        projected_ref[...] = exact(half, inv, ((1,), (1,)))

    return call(
        finish,
        (sds((rows_here, ncol), F32), sds((rows_here, ncol), F32), sds((ncol, ncol), F32)),
        in_specs=[VMEM()] * (2 + 2 * count),
        scratch=[pltpu.VMEM((rows_here, ncol), F32)],
        micros=3.0,
    )(full, *image_all, *moment_all, inverse)


def solution(mesh):
    in_specs = (
        P("rows", None),
        P("rows", None, None, None),
        P("rows", None, None),
        P("rows", None),
        P("rows", None),
    )
    out_specs = (P("rows", None), P("rows", None), P())
    return jax.shard_map(
        per_device, mesh=mesh, in_specs=in_specs, out_specs=out_specs, check_vma=False
    )
```

```python
import functools

import jax
import jax.numpy as jnp
import numpy as np
from jax import lax
from jax.experimental import pallas as pl
from jax.experimental.pallas import tpu as pltpu
from jax.sharding import PartitionSpec as P

RADIUS = 1.0
DAMPING = 0.8
CHUNKS = 4
KEEP = 1.0 - DAMPING
VMEM_LIMIT = 24 * 1024 * 1024
FIRST_LIMIT = 52 * 1024 * 1024
FLOPS_PER_MICRO = 1.1e9
GRAM_MICROS = 6.0
F32 = jnp.float32
BF16 = jnp.bfloat16


def split(value):
    high = value.astype(BF16)
    low = (value - high.astype(F32)).astype(BF16)
    return high, low


def dot(left, right):
    return jnp.dot(left, right, preferred_element_type=F32)


def dot_three(stacked, high, low):
    half = stacked.shape[0] // 2
    both = dot(stacked, high)
    return both[:half] + both[half:] + dot(stacked[:half], low)


def apply_three(stacked, value):
    return dot_three(stacked, *split(value))


def exact(left, right, contract):
    return lax.dot_general(
        left, right, (contract, ((), ())), precision=lax.Precision.HIGHEST,
        preferred_element_type=F32,
    )


def lane_group(shape, width):
    return lax.broadcasted_iota(jnp.int32, shape, len(shape) - 1) // width


def spread(value, group, width):
    kept = jnp.where(lane_group(value.shape, width) == group, value, 0.0)
    return fold(kept, width)


def fold(value, width):
    lanes = value.shape[-1]
    groups = lanes // width
    if groups & (groups - 1) == 0:
        step = lanes // 2
        while step >= width:
            value = value + pltpu.roll(value, step, value.ndim - 1)
            step //= 2
        return value
    total = value
    for k in range(1, groups):
        total = total + pltpu.roll(value, k * width, value.ndim - 1)
    return total


def column_of(row):
    n = row.shape[1]
    shape = (n, n)
    diagonal = lax.broadcasted_iota(jnp.int32, shape, 0) == lax.broadcasted_iota(jnp.int32, shape, 1)
    return jnp.sum(jnp.where(diagonal, jnp.broadcast_to(row, shape), 0.0), axis=1, keepdims=True)


def lane_table(values, shape, width):
    groups = lane_group(shape, width)
    out = jnp.full(shape, float(values[0]), F32)
    for j in range(1, len(values)):
        out = jnp.where(groups == j, float(values[j]), out)
    return out


def call(kernel, out_shape, in_specs, scratch=(), micros=1.0, limit=VMEM_LIMIT):
    single = not isinstance(out_shape, (tuple, list))
    return pl.pallas_call(
        kernel,
        out_shape=out_shape,
        in_specs=in_specs,
        out_specs=VMEM() if single else [VMEM()] * len(out_shape),
        scratch_shapes=list(scratch),
        compiler_params=pltpu.CompilerParams(vmem_limit_bytes=limit),
        cost_estimate=pl.CostEstimate(flops=int(micros * FLOPS_PER_MICRO), bytes_accessed=0, transcendentals=0),
    )


VMEM = functools.partial(pl.BlockSpec, memory_space=pltpu.VMEM)
SMEM = functools.partial(pl.BlockSpec, memory_space=pltpu.SMEM)
HBM = functools.partial(pl.BlockSpec, memory_space=pltpu.HBM)


def per_device(neighbours, couplings, eigvectors, eigvalues, start_block):
    blk_dev, blk = eigvalues.shape
    nnb = neighbours.shape[1]
    ncol = start_block.shape[1]
    rows_here = blk_dev * blk
    count = lax.axis_size("shift")
    nrows = lax.axis_size("rows")
    total = rows_here * nrows
    width = ncol // count
    packs = blk_dev // count
    wide = 2 * ncol
    here = lax.axis_index("shift")
    me = lax.axis_index("rows")
    paired = nrows % 2 == 0
    halves = 2 if count % 2 == 0 else 1
    per_half = blk_dev // halves
    half_id = here % halves

    angle = np.pi * (np.arange(count, dtype=np.float64) + 0.5) / count
    real_parts = RADIUS * np.cos(angle)
    imag_parts = RADIUS * np.sin(angle)

    def inverse_scale(energy):
        offset = lane_table(real_parts, (1, ncol), width) - energy
        imag = lane_table(imag_parts, (1, ncol), width)
        inverse = 1.0 / (offset * offset + imag * imag)
        return offset * inverse, -(imag * inverse)

    def own_group():
        return lax.axis_index("shift")

    def block_rows(i):
        return slice((i // count) * blk, (i // count + 1) * blk)

    def store_packed(ref, i, value):
        kept = jnp.where(lane_group(value.shape, width) == i % count, value, 0.0)
        if i % count == 0:
            ref[block_rows(i), :] = kept
        else:
            ref[block_rows(i), :] += kept

    def swap(value):
        if paired:
            return lax.ppermute(value, "rows", [(i, i ^ 1) for i in range(nrows)])
        return lax.ppermute(value, "rows", [(i + 1, i) for i in range(nrows - 1)])

    def pass_on(value, arrived):
        if paired:
            pairs = [(i, i + 2) for i in range(0, nrows - 2, 2)] + [(i, i - 2) for i in range(3, nrows, 2)]
            return lax.ppermute(arrived, "rows", pairs)
        return lax.ppermute(value, "rows", [(i, i + 1) for i in range(nrows - 1)])

    def after(value, *others):
        return lax.optimization_barrier((value,) + others)[0]

    def halo(values):
        first = [swap(v) for v in values]
        second = [pass_on(v, a) for v, a in zip(values, first)]
        return first, second

    def mate(value):
        return lax.ppermute(value, "shift", [(i, i ^ 1) for i in range(count)])

    def mate_rows(value, step):
        return jnp.concatenate(
            [value, lax.ppermute(value, "shift", [(i, i ^ step) for i in range(count)])], axis=0
        )

    def rest_of_pairs(value, parts):
        while parts < count:
            value = mate_rows(value, parts)
            parts *= 2
        rows_each = value.shape[0] // count
        return [value[k * rows_each:(k + 1) * rows_each] for k in range(count)]

    def gather_shift(value):
        return [value] + [
            lax.ppermute(value, "shift", [(source(i, k), i) for i in range(count)]) for k in range(1, count)
        ]

    def source(i, k):
        return i ^ k if count & (count - 1) == 0 else (i + count - k) % count

    def sum_rows(value):
        if nrows & (nrows - 1):
            return lax.psum(value, "rows")
        step = 1
        while step < nrows:
            value = value + lax.ppermute(value, "rows", [(i, i ^ step) for i in range(nrows)])
            step *= 2
        return value

    place = neighbours - (me * blk_dev - blk_dev)
    group = place // blk_dev
    partner_group = jnp.where(me % 2 == 0, 2, 0) if paired else 2
    slot = place % blk_dev + blk_dev * jnp.where(group == 1, 0, jnp.where(group == partner_group, 1, 2))
    slot = slot.astype(jnp.int32)

    lead = lax.dynamic_slice_in_dim(eigvectors, half_id * per_half, per_half, axis=0).reshape(per_half * blk, blk)

    def put(xh, xl, block, value):
        rows = pl.ds(pl.multiple_of(block * blk, blk), blk)
        h, l = split(value)
        xh[rows, :] = h
        xl[rows, :] = l

    def prepare(
        start_hbm, vec_hbm, coup_hbm, val, spun, packed, vec_st, vec_ts, scale, cst, start, vec, coup, sems
    ):
        blocks = range(blk_dev)
        copies, late = [], []
        for i in blocks:
            rows = pl.ds(i * blk, blk)
            copies.append(pltpu.make_async_copy(vec_hbm.at[i], vec.at[i], sems.at[i]))
            copies.append(pltpu.make_async_copy(start_hbm.at[rows], start.at[rows], sems.at[blk_dev + i]))
            late.append(pltpu.make_async_copy(coup_hbm.at[i], coup.at[i], sems.at[2 * blk_dev + i]))
        for copy in copies + late:
            copy.start()
        scales = [inverse_scale(column_of(val[i:i + 1, :])) for i in blocks]
        for i in blocks:
            scale[i, :, :ncol] = scales[i][0]
            scale[i, :, ncol:] = scales[i][1]
        for copy in copies:
            copy.wait()
        mine_now = own_group()
        packed[packs * blk:, :] = val[...]
        backward, rights = [], []
        for i in blocks:
            v = vec[i]
            backward.append(jnp.concatenate(split(v.T), axis=0))
            vec_st[i] = jnp.concatenate(split(v), axis=0)
            vec_ts[i] = backward[i]
            rights.append(split(spread(start[i * blk:(i + 1) * blk, :], mine_now, width)))
        turned = [dot_three(backward[i], *rights[i]) for i in blocks]
        for i in blocks:
            spun[i] = turned[i]
            store_packed(packed, i, turned[i])
        for i in blocks:
            late[i].wait()
            for k in range(nnb):
                ch, cl = split(coup[i, k])
                cst[i, :blk, k * blk:(k + 1) * blk] = ch
                cst[i, blk:, k * blk:(k + 1) * blk] = cl

    sds = jax.ShapeDtypeStruct
    spun, packed, vec_st, vec_ts, scale, cst = call(
        prepare,
        (
            sds((blk_dev, blk, ncol), F32),
            sds((packs * blk + blk_dev, ncol), F32),
            sds((blk_dev, 2 * blk, blk), BF16),
            sds((blk_dev, 2 * blk, blk), BF16),
            sds((blk_dev, blk, wide), F32),
            sds((blk_dev, 2 * blk, nnb * blk), BF16),
        ),
        in_specs=[HBM()] * 3 + [VMEM()],
        scratch=[
            pltpu.VMEM((rows_here, ncol), F32), pltpu.VMEM((blk_dev, blk, blk), F32),
            pltpu.VMEM((blk_dev, nnb, blk, blk), F32), pltpu.SemaphoreType.DMA((3 * blk_dev,)),
        ],
        micros=20.0, limit=FIRST_LIMIT,
    )(start_block, eigvectors, couplings, eigvalues)

    lead_first = after(swap(lead), packed)
    pack_first = swap(after(packed, lead_first))
    lead_second = pass_on(lead, lead_first)
    pack_second = pass_on(packed, pack_first)

    mate_first = [mate(after(lead_first, pack_first))] if halves == 2 else []

    def fill_first(inputs, xh, xl, offset):
        pack = inputs[0]
        names, lefts, rights = [], [], []
        for h in range(halves):
            base = ((lax.axis_index("shift") + h) % halves) * per_half if halves > 1 else 0
            for j in range(per_half):
                b = base + j
                row0 = pl.multiple_of((b // count) * blk, blk)
                turned = spread(pack[pl.ds(row0, blk), :], b % count, width) * DAMPING
                re, im = inverse_scale(column_of(pack[pl.ds(packs * blk + b, 1), :]))
                vector = inputs[1 + h][j * blk:(j + 1) * blk, :]
                names.append(b)
                lefts.append(jnp.concatenate(split(vector), axis=0))
                rights.append(jnp.concatenate([re * turned, im * turned], axis=1))
        fields = [apply_three(left, right) for left, right in zip(lefts, rights)]
        for b, field in zip(names, fields):
            put(xh, xl, b + offset, field)

    partners = [pack_first, lead_first] + mate_first

    def first_two(*refs):
        spun_ref, scale_ref, vec = refs[:3]
        inputs = refs[3:3 + len(partners)]
        xh, xl = refs[3 + len(partners):]
        firsts = []
        for i in range(blk_dev):
            turned = DAMPING * spun_ref[i]
            s = scale_ref[i]
            firsts.append(jnp.concatenate([s[:, :ncol] * turned, s[:, ncol:] * turned], axis=1))
        fields = [apply_three(vec[i], firsts[i]) for i in range(blk_dev)]
        for i in range(blk_dev):
            put(xh, xl, i, fields[i])
        fill_first(inputs, xh, xl, blk_dev)

    two_shape = (sds((2 * rows_here, wide), BF16), sds((2 * rows_here, wide), BF16))
    two_h, two_l = call(
        first_two, two_shape, in_specs=[VMEM()] * (3 + len(partners)), micros=2.0,
    )(spun, scale, vec_st, *partners)

    def near_of(ref, slots, i):
        return jnp.concatenate(
            [ref[pl.ds(pl.multiple_of(slots[i, k] * blk, blk), blk), :] for k in range(nnb)], axis=0
        )

    def coupled(slots, c, xh, xl, i):
        return dot_three(c[i], near_of(xh, slots, i), near_of(xl, slots, i))

    def times(s, g):
        re, im = g[:, :ncol], g[:, ncol:]
        sre, sim = s[:, :ncol], s[:, ncol:]
        return jnp.concatenate([sre * re - sim * im, sre * im + sim * re], axis=1)

    def plus_real(g, b):
        return jnp.concatenate([g[:, :ncol] + b, g[:, ncol:]], axis=1)

    sizes = [blk_dev // CHUNKS] * CHUNKS if blk_dev % CHUNKS == 0 else [blk_dev]
    chunks = len(sizes)
    spots = [(c, j) for c in range(chunks) for j in range(sizes[c])]

    mate_second = [mate(after(lead_second, pack_second))] if halves == 2 else []
    others = [pack_second, lead_second] + mate_second

    def second_iterate(*refs):
        slots, th, tl, c, vec, vec_t, spun_ref, scale_ref = refs[:8]
        inputs = refs[8:8 + len(others)]
        outs = refs[8 + len(others):8 + len(others) + chunks]
        hats, xh, xl = refs[8 + len(others) + chunks:]
        fill_first(inputs, xh, xl, 2 * blk_dev)
        xh[:2 * rows_here, :] = th[...]
        xl[:2 * rows_here, :] = tl[...]
        blocks = range(blk_dev)
        sums = [coupled(slots, c, xh, xl, i) for i in blocks]
        turned = [apply_three(vec_t[i], sums[i]) for i in blocks]
        for i in blocks:
            hats[i] = times(scale_ref[i], DAMPING * plus_real(turned[i], (1.0 + KEEP) * spun_ref[i]))
        result = [apply_three(vec[i], hats[i]) for i in blocks]
        for i in blocks:
            q, j = spots[i]
            outs[q][j] = result[i]

    field_scratch = [pltpu.VMEM((3 * rows_here, wide), BF16)] * 2
    *own, hats = call(
        second_iterate,
        [sds((size, blk, wide), F32) for size in sizes] + [sds((blk_dev, blk, wide), F32)],
        in_specs=[SMEM()] + [VMEM()] * (7 + len(others)),
        scratch=field_scratch,
        micros=6.0,
    )(slot, two_h, two_l, cst, vec_st, vec_ts, spun, scale, *others)

    two_first, two_second = halo(own)

    def third_iterate(*refs):
        slots = refs[0]
        fields = refs[1:1 + 3 * chunks]
        hats_ref, c, vec, vec_t, spun_ref, scale_ref, val = refs[1 + 3 * chunks:8 + 3 * chunks]
        packed_out, diag_out, xh, xl = refs[8 + 3 * chunks:]
        for side in range(3):
            for i, (q, j) in enumerate(spots):
                put(xh, xl, side * blk_dev + i, fields[side * chunks + q][j])
        weight_re = lane_table(real_parts / count, (1, ncol), width)
        weight_im = lane_table(imag_parts / count, (1, ncol), width)
        blocks = range(blk_dev)
        sums = [coupled(slots, c, xh, xl, i) for i in blocks]
        turned = [apply_three(vec_t[i], sums[i]) for i in blocks]
        ends = []
        for i in blocks:
            hat = KEEP * hats_ref[i] + times(scale_ref[i], DAMPING * plus_real(turned[i], spun_ref[i]))
            term = fold(weight_re * hat[:, :ncol] - weight_im * hat[:, ncol:], width)
            energy = column_of(val[i:i + 1, :])
            ends.append(jnp.concatenate([term, energy * term], axis=1))
        result = [apply_three(vec[i], ends[i]) for i in blocks]
        for i in blocks:
            diag_out[i] = result[i][:, ncol:]
            store_packed(packed_out, i, result[i][:, :ncol])

    filtered, diagonal = call(
        third_iterate,
        (sds((packs * blk, ncol), F32), sds((blk_dev, blk, ncol), F32)),
        in_specs=[SMEM()] + [VMEM()] * (7 + 3 * chunks),
        scratch=field_scratch,
        micros=6.0,
    )(slot, *own, *two_first, *two_second, hats, cst, vec_st, vec_ts, spun, scale, eigvalues)

    (filt_first,), (filt_second,) = halo([filtered])
    filt_all = gather_shift(filtered)

    def unpacked(refs, rows, g):
        lanes = lane_group((rows.stop - rows.start, ncol), width)
        out = jnp.zeros(lanes.shape, F32)
        mine_now = own_group()
        for k, ref in enumerate(refs):
            s = source(mine_now, k) if k else mine_now
            moved = pltpu.roll(ref[rows, :], ((s - g + count) % count) * width, 1)
            out = jnp.where(lanes == s, moved, out)
        return out

    def gram_of(*refs):
        pieces, full, gram = refs[:count], refs[count], refs[1 + count]
        for i in range(blk_dev):
            full[i * blk:(i + 1) * blk, :] = unpacked(pieces, block_rows(i), i % count)
        gram[...] = exact(full[...], full[...], ((0,), (0,)))

    full, gram = call(
        gram_of,
        (sds((rows_here, ncol), F32), sds((ncol, ncol), F32)),
        in_specs=[VMEM()] * count,
        micros=GRAM_MICROS,
    )(*filt_all)

    span = ncol // count

    def image_of(slots, own_f, first_f, second_f, full_ref, c, diag, joined, xh, xl, image_ref):
        for f, field in enumerate((own_f, first_f, second_f)):
            for b in range(blk_dev):
                put(xh, xl, f * blk_dev + b, spread(field[block_rows(b), :], b % count, width))
        for i in range(blk_dev):
            image = diag[i] + coupled(slots, c, xh, xl, i)
            image_ref[i * blk:(i + 1) * blk, :] = image
            store_packed(joined, i, image)
        part = exact(full_ref[...], image_ref[...], ((0,), (0,)))
        piece = jnp.zeros((span, ncol), F32)
        for s in range(count):
            piece = piece + jnp.where(
                lane_group((span, ncol), width) == s, part[s * span:(s + 1) * span, :], 0.0
            )
        joined[packs * blk:, :] = piece

    joined = call(
        image_of,
        sds((packs * blk + span, ncol), F32),
        in_specs=[SMEM()] + [VMEM()] * 6,
        scratch=[pltpu.VMEM((3 * rows_here, ncol), BF16)] * 2 + [pltpu.VMEM((rows_here, ncol), F32)],
        micros=3.8,
    )(slot, filtered, filt_first, filt_second, full, cst, diagonal)

    if count & (count - 1):
        pieces, parts = gather_shift(joined), count
    else:
        parts = min(2, count)
        both = mate_rows(joined, 1) if parts == 2 else joined
        pieces = [both[k * (packs * blk + span):(k + 1) * (packs * blk + span)] for k in range(parts)]
    sums = sum_rows(jnp.concatenate([gram] + [piece[packs * blk:] for piece in pieces], axis=0))
    image_all = rest_of_pairs(jnp.concatenate([piece[:packs * blk] for piece in pieces], axis=0), parts)
    moment_all = rest_of_pairs(sums[ncol:], parts)

    def factor_of(*refs):
        sums_ref, full_ref, pieces = refs[0], refs[1], refs[2:2 + count]
        inverse, basis_ref, image_ref, raw = refs[2 + count:]
        tiles = ncol // 8
        a = [sums_ref[t * 8:(t + 1) * 8, :] * (1.0 / total) for t in range(tiles)]
        lanes = lax.broadcasted_iota(jnp.int32, (8, ncol), 1)
        subs = lax.broadcasted_iota(jnp.int32, (8, ncol), 0)
        e = [jnp.where(lanes == subs + t * 8, 1.0, 0.0).astype(F32) for t in range(tiles)]
        for t in range(tiles):
            below = range(t, tiles)
            cols = [
                {u: jnp.broadcast_to(a[u][:, t * 8 + j:t * 8 + j + 1], (8, ncol)) for u in below} for j in range(8)
            ]
            rows = [a[t][j:j + 1, :] for j in range(8)]
            erows = [e[t][j:j + 1, :] for j in range(8)]
            factors = []
            for j in range(8):
                inv = 1.0 / cols[j][t][j:j + 1, :]
                m = {u: cols[j][u] * inv for u in below}
                m[t] = jnp.where(subs > j, m[t], 0.0)
                for q in range(j + 1, 8):
                    above = cols[q][t][j:j + 1, :]
                    for u in below:
                        cols[q][u] = cols[q][u] - m[u] * above
                    left = m[t][q:q + 1, :]
                    rows[q] = rows[q] - left * rows[j]
                    erows[q] = erows[q] - left * erows[j]
                factors.append(m)
            for u in below:
                for j in range(8):
                    a[u] = a[u] - factors[j][u] * rows[j]
                    e[u] = e[u] - factors[j][u] * erows[j]
        for t in range(tiles):
            pivot = jnp.sum(jnp.where(lanes == subs + t * 8, a[t], 0.0), axis=1, keepdims=True)
            inverse[t * 8:(t + 1) * 8, :] = e[t] * (1.0 / jnp.sqrt(pivot))

        inv = inverse[...]
        for i in range(blk_dev):
            raw[i * blk:(i + 1) * blk, :] = unpacked(pieces, block_rows(i), i % count)
        basis_ref[...] = exact(full_ref[...], inv, ((1,), (1,)))
        image_ref[...] = exact(raw[...], inv, ((1,), (1,)))

    inverse, basis, basis_image = call(
        factor_of,
        (sds((ncol, ncol), F32), sds((rows_here, ncol), F32), sds((rows_here, ncol), F32)),
        in_specs=[VMEM()] * (2 + count),
        scratch=[pltpu.VMEM((rows_here, ncol), F32)],
        micros=7.0,
    )(sums, full, *image_all)

    def project(*refs):
        moments, inv_ref, projected_ref = refs[:count], refs[count], refs[count + 1]
        inv = inv_ref[...]
        strips = [unpacked(moments, slice(0, span), g) for g in range(count)]
        m = jnp.concatenate(strips, axis=0) * (1.0 / total)
        projected_ref[...] = exact(exact(inv, m, ((1,), (0,))), inv, ((1,), (1,)))

    projected = call(
        project, sds((ncol, ncol), F32), in_specs=[VMEM()] * (count + 1), micros=1.0,
    )(*moment_all, inverse)
    return (basis, basis_image, projected)


def solution(mesh):
    in_specs = (
        P("rows", None),
        P("rows", None, None, None),
        P("rows", None, None),
        P("rows", None),
        P("rows", None),
    )
    out_specs = (P("rows", None), P("rows", None), P())
    return jax.shard_map(
        per_device, mesh=mesh, in_specs=in_specs, out_specs=out_specs, check_vma=False
    )
```

```python
import functools

import jax
import jax.numpy as jnp
import numpy as np
from jax import lax
from jax.experimental import pallas as pl
from jax.experimental.pallas import tpu as pltpu
from jax.sharding import PartitionSpec as P

RADIUS = 1.0
DAMPING = 0.8
CHUNKS = 4
KEEP = 1.0 - DAMPING
VMEM_LIMIT = 24 * 1024 * 1024
FIRST_LIMIT = 52 * 1024 * 1024
FLOPS_PER_MICRO = 1.1e9
GRAM_MICROS = 6.0
F32 = jnp.float32
BF16 = jnp.bfloat16


def split(value):
    high = value.astype(BF16)
    low = (value - high.astype(F32)).astype(BF16)
    return high, low


def dot(left, right):
    return jnp.dot(left, right, preferred_element_type=F32)


def dot_three(stacked, high, low):
    half = stacked.shape[0] // 2
    both = dot(stacked, high)
    return both[:half] + both[half:] + dot(stacked[:half], low)


def apply_three(stacked, value):
    return dot_three(stacked, *split(value))


def exact(left, right, contract):
    return lax.dot_general(
        left, right, (contract, ((), ())), precision=lax.Precision.HIGHEST,
        preferred_element_type=F32,
    )


def lane_group(shape, width):
    return lax.broadcasted_iota(jnp.int32, shape, len(shape) - 1) // width


def spread(value, group, width):
    kept = jnp.where(lane_group(value.shape, width) == group, value, 0.0)
    return fold(kept, width)


def fold(value, width):
    lanes = value.shape[-1]
    groups = lanes // width
    if groups & (groups - 1) == 0:
        step = lanes // 2
        while step >= width:
            value = value + pltpu.roll(value, step, value.ndim - 1)
            step //= 2
        return value
    total = value
    for k in range(1, groups):
        total = total + pltpu.roll(value, k * width, value.ndim - 1)
    return total


def column_of(row):
    n = row.shape[1]
    shape = (n, n)
    diagonal = lax.broadcasted_iota(jnp.int32, shape, 0) == lax.broadcasted_iota(jnp.int32, shape, 1)
    return jnp.sum(jnp.where(diagonal, jnp.broadcast_to(row, shape), 0.0), axis=1, keepdims=True)


def lane_table(values, shape, width):
    groups = lane_group(shape, width)
    out = jnp.full(shape, float(values[0]), F32)
    for j in range(1, len(values)):
        out = jnp.where(groups == j, float(values[j]), out)
    return out


def call(kernel, out_shape, in_specs, scratch=(), micros=1.0, limit=VMEM_LIMIT):
    single = not isinstance(out_shape, (tuple, list))
    return pl.pallas_call(
        kernel,
        out_shape=out_shape,
        in_specs=in_specs,
        out_specs=VMEM() if single else [VMEM()] * len(out_shape),
        scratch_shapes=list(scratch),
        compiler_params=pltpu.CompilerParams(vmem_limit_bytes=limit),
        cost_estimate=pl.CostEstimate(flops=int(micros * FLOPS_PER_MICRO), bytes_accessed=0, transcendentals=0),
    )


VMEM = functools.partial(pl.BlockSpec, memory_space=pltpu.VMEM)
SMEM = functools.partial(pl.BlockSpec, memory_space=pltpu.SMEM)
HBM = functools.partial(pl.BlockSpec, memory_space=pltpu.HBM)


def per_device(neighbours, couplings, eigvectors, eigvalues, start_block):
    blk_dev, blk = eigvalues.shape
    nnb = neighbours.shape[1]
    ncol = start_block.shape[1]
    rows_here = blk_dev * blk
    count = lax.axis_size("shift")
    nrows = lax.axis_size("rows")
    total = rows_here * nrows
    width = ncol // count
    packs = blk_dev // count
    wide = 2 * ncol
    here = lax.axis_index("shift")
    me = lax.axis_index("rows")
    paired = nrows % 2 == 0
    halves = 2 if count % 2 == 0 else 1
    per_half = blk_dev // halves
    half_id = here % halves

    angle = np.pi * (np.arange(count, dtype=np.float64) + 0.5) / count
    real_parts = RADIUS * np.cos(angle)
    imag_parts = RADIUS * np.sin(angle)

    def inverse_scale(energy):
        offset = lane_table(real_parts, (1, ncol), width) - energy
        imag = lane_table(imag_parts, (1, ncol), width)
        inverse = 1.0 / (offset * offset + imag * imag)
        return offset * inverse, -(imag * inverse)

    def own_group():
        return lax.axis_index("shift")

    def block_rows(i):
        return slice((i // count) * blk, (i // count + 1) * blk)

    def store_packed(ref, i, value):
        kept = jnp.where(lane_group(value.shape, width) == i % count, value, 0.0)
        if i % count == 0:
            ref[block_rows(i), :] = kept
        else:
            ref[block_rows(i), :] += kept

    def swap(value):
        if paired:
            return lax.ppermute(value, "rows", [(i, i ^ 1) for i in range(nrows)])
        return lax.ppermute(value, "rows", [(i + 1, i) for i in range(nrows - 1)])

    def pass_on(value, arrived):
        if paired:
            pairs = [(i, i + 2) for i in range(0, nrows - 2, 2)] + [(i, i - 2) for i in range(3, nrows, 2)]
            return lax.ppermute(arrived, "rows", pairs)
        return lax.ppermute(value, "rows", [(i, i + 1) for i in range(nrows - 1)])

    def after(value, *others):
        return lax.optimization_barrier((value,) + others)[0]

    def halo(values):
        first = [swap(v) for v in values]
        second = [pass_on(v, a) for v, a in zip(values, first)]
        return first, second

    def mate(value):
        return lax.ppermute(value, "shift", [(i, i ^ 1) for i in range(count)])

    def mate_rows(value, step):
        return jnp.concatenate(
            [value, lax.ppermute(value, "shift", [(i, i ^ step) for i in range(count)])], axis=0
        )

    def rest_of_pairs(value, parts):
        while parts < count:
            value = mate_rows(value, parts)
            parts *= 2
        rows_each = value.shape[0] // count
        return [value[k * rows_each:(k + 1) * rows_each] for k in range(count)]

    def gather_shift(value):
        return [value] + [
            lax.ppermute(value, "shift", [(source(i, k), i) for i in range(count)]) for k in range(1, count)
        ]

    def source(i, k):
        return i ^ k if count & (count - 1) == 0 else (i + count - k) % count

    def sum_rows(value):
        if nrows & (nrows - 1):
            return lax.psum(value, "rows")
        step = 1
        while step < nrows:
            value = value + lax.ppermute(value, "rows", [(i, i ^ step) for i in range(nrows)])
            step *= 2
        return value

    place = neighbours - (me * blk_dev - blk_dev)
    group = place // blk_dev
    partner_group = jnp.where(me % 2 == 0, 2, 0) if paired else 2
    slot = place % blk_dev + blk_dev * jnp.where(group == 1, 0, jnp.where(group == partner_group, 1, 2))
    slot = slot.astype(jnp.int32)

    lead = lax.dynamic_slice_in_dim(eigvectors, half_id * per_half, per_half, axis=0).reshape(per_half * blk, blk)

    def put(xh, xl, block, value):
        rows = pl.ds(pl.multiple_of(block * blk, blk), blk)
        h, l = split(value)
        xh[rows, :] = h
        xl[rows, :] = l

    def prepare(
        start_hbm, vec_hbm, coup_hbm, val, spun, packed, vec_st, vec_ts, cst, start, vec, coup, sems
    ):
        blocks = range(blk_dev)
        copies, late = [], []
        for i in blocks:
            rows = pl.ds(i * blk, blk)
            copies.append(pltpu.make_async_copy(vec_hbm.at[i], vec.at[i], sems.at[i]))
            copies.append(pltpu.make_async_copy(start_hbm.at[rows], start.at[rows], sems.at[blk_dev + i]))
            late.append(pltpu.make_async_copy(coup_hbm.at[i], coup.at[i], sems.at[2 * blk_dev + i]))
        for copy in copies + late:
            copy.start()
        for copy in copies:
            copy.wait()
        mine_now = own_group()
        packed[packs * blk:, :] = val[...]
        backward, rights = [], []
        for i in blocks:
            v = vec[i]
            backward.append(jnp.concatenate(split(v.T), axis=0))
            vec_st[i] = jnp.concatenate(split(v), axis=0)
            vec_ts[i] = backward[i]
            rights.append(split(spread(start[i * blk:(i + 1) * blk, :], mine_now, width)))
        turned = [dot_three(backward[i], *rights[i]) for i in blocks]
        for i in blocks:
            spun[i] = turned[i]
            store_packed(packed, i, turned[i])
        for i in blocks:
            late[i].wait()
            for k in range(nnb):
                ch, cl = split(coup[i, k])
                cst[i, :blk, k * blk:(k + 1) * blk] = ch
                cst[i, blk:, k * blk:(k + 1) * blk] = cl

    sds = jax.ShapeDtypeStruct
    spun, packed, vec_st, vec_ts, cst = call(
        prepare,
        (
            sds((blk_dev, blk, ncol), F32),
            sds((packs * blk + blk_dev, ncol), F32),
            sds((blk_dev, 2 * blk, blk), BF16),
            sds((blk_dev, 2 * blk, blk), BF16),
            sds((blk_dev, 2 * blk, nnb * blk), BF16),
        ),
        in_specs=[HBM()] * 3 + [VMEM()],
        scratch=[
            pltpu.VMEM((rows_here, ncol), F32), pltpu.VMEM((blk_dev, blk, blk), F32),
            pltpu.VMEM((blk_dev, nnb, blk, blk), F32), pltpu.SemaphoreType.DMA((3 * blk_dev,)),
        ],
        micros=20.0, limit=FIRST_LIMIT,
    )(start_block, eigvectors, couplings, eigvalues)

    lead_first = after(swap(lead), packed)
    pack_first = swap(after(packed, lead_first))
    lead_second = pass_on(lead, lead_first)
    pack_second = pass_on(packed, pack_first)

    mate_first = [mate(after(lead_first, pack_first))] if halves == 2 else []

    def fill_first(inputs, xh, xl, offset):
        pack = inputs[0]
        names, lefts, rights = [], [], []
        for h in range(halves):
            base = ((lax.axis_index("shift") + h) % halves) * per_half if halves > 1 else 0
            for j in range(per_half):
                b = base + j
                row0 = pl.multiple_of((b // count) * blk, blk)
                turned = spread(pack[pl.ds(row0, blk), :], b % count, width) * DAMPING
                re, im = inverse_scale(column_of(pack[pl.ds(packs * blk + b, 1), :]))
                vector = inputs[1 + h][j * blk:(j + 1) * blk, :]
                names.append(b)
                lefts.append(jnp.concatenate(split(vector), axis=0))
                rights.append(jnp.concatenate([re * turned, im * turned], axis=1))
        fields = [apply_three(left, right) for left, right in zip(lefts, rights)]
        for b, field in zip(names, fields):
            put(xh, xl, b + offset, field)

    partners = [pack_first, lead_first] + mate_first

    def first_two(*refs):
        spun_ref, val, vec = refs[:3]
        inputs = refs[3:3 + len(partners)]
        xh, xl, scale = refs[3 + len(partners):]
        firsts = []
        for i in range(blk_dev):
            turned = DAMPING * spun_ref[i]
            re, im = inverse_scale(column_of(val[i:i + 1, :]))
            scale[i, :, :ncol] = re
            scale[i, :, ncol:] = im
            firsts.append(jnp.concatenate([re * turned, im * turned], axis=1))
        fields = [apply_three(vec[i], firsts[i]) for i in range(blk_dev)]
        for i in range(blk_dev):
            put(xh, xl, i, fields[i])
        fill_first(inputs, xh, xl, blk_dev)

    two_shape = (sds((2 * rows_here, wide), BF16),) * 2 + (sds((blk_dev, blk, wide), F32),)
    two_h, two_l, scale = call(
        first_two, two_shape, in_specs=[VMEM()] * (3 + len(partners)), micros=2.0,
    )(spun, eigvalues, vec_st, *partners)

    def near_of(ref, slots, i):
        return jnp.concatenate(
            [ref[pl.ds(pl.multiple_of(slots[i, k] * blk, blk), blk), :] for k in range(nnb)], axis=0
        )

    def coupled(slots, c, xh, xl, i):
        return dot_three(c[i], near_of(xh, slots, i), near_of(xl, slots, i))

    def times(s, g):
        re, im = g[:, :ncol], g[:, ncol:]
        sre, sim = s[:, :ncol], s[:, ncol:]
        return jnp.concatenate([sre * re - sim * im, sre * im + sim * re], axis=1)

    def plus_real(g, b):
        return jnp.concatenate([g[:, :ncol] + b, g[:, ncol:]], axis=1)

    sizes = [blk_dev // CHUNKS] * CHUNKS if blk_dev % CHUNKS == 0 else [blk_dev]
    chunks = len(sizes)
    spots = [(c, j) for c in range(chunks) for j in range(sizes[c])]

    mate_second = [mate(after(lead_second, pack_second))] if halves == 2 else []
    others = [pack_second, lead_second] + mate_second

    def second_iterate(*refs):
        slots, th, tl, c, vec, vec_t, spun_ref, scale_ref = refs[:8]
        inputs = refs[8:8 + len(others)]
        outs = refs[8 + len(others):8 + len(others) + chunks]
        hats, xh, xl = refs[8 + len(others) + chunks:]
        fill_first(inputs, xh, xl, 2 * blk_dev)
        xh[:2 * rows_here, :] = th[...]
        xl[:2 * rows_here, :] = tl[...]
        blocks = range(blk_dev)
        sums = [coupled(slots, c, xh, xl, i) for i in blocks]
        turned = [apply_three(vec_t[i], sums[i]) for i in blocks]
        for i in blocks:
            hats[i] = times(scale_ref[i], DAMPING * plus_real(turned[i], (1.0 + KEEP) * spun_ref[i]))
        result = [apply_three(vec[i], hats[i]) for i in blocks]
        for i in blocks:
            q, j = spots[i]
            outs[q][j] = result[i]

    field_scratch = [pltpu.VMEM((3 * rows_here, wide), BF16)] * 2
    *own, hats = call(
        second_iterate,
        [sds((size, blk, wide), F32) for size in sizes] + [sds((blk_dev, blk, wide), F32)],
        in_specs=[SMEM()] + [VMEM()] * (7 + len(others)),
        scratch=field_scratch,
        micros=6.0,
    )(slot, two_h, two_l, cst, vec_st, vec_ts, spun, scale, *others)

    two_first, two_second = halo(own)

    def third_iterate(*refs):
        slots = refs[0]
        fields = refs[1:1 + 3 * chunks]
        hats_ref, c, vec, vec_t, spun_ref, scale_ref, val = refs[1 + 3 * chunks:8 + 3 * chunks]
        packed_out, diag_out, xh, xl = refs[8 + 3 * chunks:]
        for side in range(3):
            for i, (q, j) in enumerate(spots):
                put(xh, xl, side * blk_dev + i, fields[side * chunks + q][j])
        weight_re = lane_table(real_parts / count, (1, ncol), width)
        weight_im = lane_table(imag_parts / count, (1, ncol), width)
        blocks = range(blk_dev)
        sums = [coupled(slots, c, xh, xl, i) for i in blocks]
        turned = [apply_three(vec_t[i], sums[i]) for i in blocks]
        ends = []
        for i in blocks:
            hat = KEEP * hats_ref[i] + times(scale_ref[i], DAMPING * plus_real(turned[i], spun_ref[i]))
            term = fold(weight_re * hat[:, :ncol] - weight_im * hat[:, ncol:], width)
            energy = column_of(val[i:i + 1, :])
            ends.append(jnp.concatenate([term, energy * term], axis=1))
        result = [apply_three(vec[i], ends[i]) for i in blocks]
        for i in blocks:
            diag_out[i] = result[i][:, ncol:]
            store_packed(packed_out, i, result[i][:, :ncol])

    filtered, diagonal = call(
        third_iterate,
        (sds((packs * blk, ncol), F32), sds((blk_dev, blk, ncol), F32)),
        in_specs=[SMEM()] + [VMEM()] * (7 + 3 * chunks),
        scratch=field_scratch,
        micros=6.0,
    )(slot, *own, *two_first, *two_second, hats, cst, vec_st, vec_ts, spun, scale, eigvalues)

    (filt_first,), (filt_second,) = halo([filtered])
    filt_all = gather_shift(filtered)

    def unpacked(refs, rows, g):
        lanes = lane_group((rows.stop - rows.start, ncol), width)
        out = jnp.zeros(lanes.shape, F32)
        mine_now = own_group()
        for k, ref in enumerate(refs):
            s = source(mine_now, k) if k else mine_now
            moved = pltpu.roll(ref[rows, :], ((s - g + count) % count) * width, 1)
            out = jnp.where(lanes == s, moved, out)
        return out

    half_col = ncol // 2

    def triangle(gram):
        top, low = gram[:half_col, :], gram[half_col:, :]
        lanes = lax.broadcasted_iota(jnp.int32, top.shape, 1)
        rows = lax.broadcasted_iota(jnp.int32, top.shape, 0)
        body = jnp.where(lanes - half_col >= rows, low, pltpu.roll(top, half_col, 1))
        diagonal = jnp.sum(jnp.where(lanes == rows, top, 0.0), axis=0, keepdims=True)
        return body, jnp.broadcast_to(diagonal, (8, ncol))

    def whole_of(body, diagonal):
        lanes = lax.broadcasted_iota(jnp.int32, body.shape, 1)
        rows = lax.broadcasted_iota(jnp.int32, body.shape, 0)
        moved = pltpu.roll(body, half_col, 1)
        top = jnp.where((lanes < rows) | (lanes >= half_col), moved, jnp.where(lanes == rows, 0.5 * diagonal, 0.0))
        past = lanes - half_col
        low = jnp.where(past > rows, body, jnp.where(past == rows, 0.5 * body, 0.0))
        both = jnp.concatenate([top, low], axis=0)
        return both + both.T

    def gram_of(*refs):
        pieces, full, gram = refs[:count], refs[count], refs[1 + count]
        for i in range(blk_dev):
            full[i * blk:(i + 1) * blk, :] = unpacked(pieces, block_rows(i), i % count)
        body, diagonal = triangle(exact(full[...], full[...], ((0,), (0,))))
        gram[:half_col, :] = body
        gram[half_col:, :] = diagonal

    full, gram = call(
        gram_of,
        (sds((rows_here, ncol), F32), sds((half_col + 8, ncol), F32)),
        in_specs=[VMEM()] * count,
        micros=GRAM_MICROS,
    )(*filt_all)

    span = ncol // count

    def image_of(slots, own_f, first_f, second_f, full_ref, c, diag, joined, xh, xl, image_ref):
        for f, field in enumerate((own_f, first_f, second_f)):
            for b in range(blk_dev):
                put(xh, xl, f * blk_dev + b, spread(field[block_rows(b), :], b % count, width))
        for i in range(blk_dev):
            image = diag[i] + coupled(slots, c, xh, xl, i)
            image_ref[i * blk:(i + 1) * blk, :] = image
            store_packed(joined, i, image)
        part = exact(full_ref[...], image_ref[...], ((0,), (0,)))
        piece = jnp.zeros((span, ncol), F32)
        for s in range(count):
            piece = piece + jnp.where(
                lane_group((span, ncol), width) == s, part[s * span:(s + 1) * span, :], 0.0
            )
        joined[packs * blk:, :] = piece

    joined = call(
        image_of,
        sds((packs * blk + span, ncol), F32),
        in_specs=[SMEM()] + [VMEM()] * 6,
        scratch=[pltpu.VMEM((3 * rows_here, ncol), BF16)] * 2 + [pltpu.VMEM((rows_here, ncol), F32)],
        micros=3.8,
    )(slot, filtered, filt_first, filt_second, full, cst, diagonal)

    if count & (count - 1):
        pieces, parts = gather_shift(joined), count
    else:
        parts = min(2, count)
        both = mate_rows(joined, 1) if parts == 2 else joined
        pieces = [both[k * (packs * blk + span):(k + 1) * (packs * blk + span)] for k in range(parts)]
    sums = sum_rows(jnp.concatenate([gram] + [piece[packs * blk:] for piece in pieces], axis=0))
    image_all = rest_of_pairs(jnp.concatenate([piece[:packs * blk] for piece in pieces], axis=0), parts)
    moment_all = rest_of_pairs(after(sums[half_col + 8:], *image_all), parts)

    def factor_of(*refs):
        sums_ref, full_ref, pieces = refs[0], refs[1], refs[2:2 + count]
        inverse, basis_ref, image_ref, raw = refs[2 + count:]
        tiles = ncol // 8
        gram_now = whole_of(sums_ref[:half_col, :], sums_ref[half_col:half_col + 1, :]) * (1.0 / total)
        a = [gram_now[t * 8:(t + 1) * 8, :] for t in range(tiles)]
        lanes = lax.broadcasted_iota(jnp.int32, (8, ncol), 1)
        subs = lax.broadcasted_iota(jnp.int32, (8, ncol), 0)
        e = [jnp.where(lanes == subs + t * 8, 1.0, 0.0).astype(F32) for t in range(tiles)]
        for t in range(tiles):
            below = range(t, tiles)
            cols = [
                {u: jnp.broadcast_to(a[u][:, t * 8 + j:t * 8 + j + 1], (8, ncol)) for u in below} for j in range(8)
            ]
            rows = [a[t][j:j + 1, :] for j in range(8)]
            erows = [e[t][j:j + 1, :] for j in range(8)]
            factors = []
            for j in range(8):
                inv = 1.0 / cols[j][t][j:j + 1, :]
                m = {u: cols[j][u] * inv for u in below}
                m[t] = jnp.where(subs > j, m[t], 0.0)
                for q in range(j + 1, 8):
                    above = cols[q][t][j:j + 1, :]
                    for u in below:
                        cols[q][u] = cols[q][u] - m[u] * above
                    left = m[t][q:q + 1, :]
                    rows[q] = rows[q] - left * rows[j]
                    erows[q] = erows[q] - left * erows[j]
                factors.append(m)
            for u in below:
                for j in range(8):
                    a[u] = a[u] - factors[j][u] * rows[j]
                    e[u] = e[u] - factors[j][u] * erows[j]
        for t in range(tiles):
            pivot = jnp.sum(jnp.where(lanes == subs + t * 8, a[t], 0.0), axis=1, keepdims=True)
            inverse[t * 8:(t + 1) * 8, :] = e[t] * (1.0 / jnp.sqrt(pivot))

        inv = inverse[...]
        for i in range(blk_dev):
            raw[i * blk:(i + 1) * blk, :] = unpacked(pieces, block_rows(i), i % count)
        basis_ref[...] = exact(full_ref[...], inv, ((1,), (1,)))
        image_ref[...] = exact(raw[...], inv, ((1,), (1,)))

    inverse, basis, basis_image = call(
        factor_of,
        (sds((ncol, ncol), F32), sds((rows_here, ncol), F32), sds((rows_here, ncol), F32)),
        in_specs=[VMEM()] * (2 + count),
        scratch=[pltpu.VMEM((rows_here, ncol), F32)],
        micros=0.5,
    )(sums, full, *image_all)

    def project(*refs):
        moments, inv_ref, projected_ref = refs[:count], refs[count], refs[count + 1]
        inv = inv_ref[...]
        strips = [unpacked(moments, slice(0, span), g) for g in range(count)]
        m = jnp.concatenate(strips, axis=0) * (1.0 / total)
        projected_ref[...] = exact(exact(inv, m, ((1,), (0,))), inv, ((1,), (1,)))

    projected = call(
        project, sds((ncol, ncol), F32), in_specs=[VMEM()] * (count + 1), micros=1.0,
    )(*moment_all, inverse)
    return (basis, basis_image, projected)


def solution(mesh):
    in_specs = (
        P("rows", None),
        P("rows", None, None, None),
        P("rows", None, None),
        P("rows", None),
        P("rows", None),
    )
    out_specs = (P("rows", None), P("rows", None), P())
    return jax.shard_map(
        per_device, mesh=mesh, in_specs=in_specs, out_specs=out_specs, check_vma=False
    )
```

```python
import functools

import jax
import jax.numpy as jnp
import numpy as np
from jax import lax
from jax.experimental import pallas as pl
from jax.experimental.pallas import tpu as pltpu
from jax.sharding import PartitionSpec as P

RADIUS = 1.0
DAMPING = 0.8
CHUNKS = 4
KEEP = 1.0 - DAMPING
VMEM_LIMIT = 24 * 1024 * 1024
FIRST_LIMIT = 52 * 1024 * 1024
FLOPS_PER_MICRO = 1.1e9
GRAM_MICROS = 6.0
F32 = jnp.float32
BF16 = jnp.bfloat16


def split(value):
    high = value.astype(BF16)
    low = (value - high.astype(F32)).astype(BF16)
    return high, low


def dot(left, right):
    return jnp.dot(left, right, preferred_element_type=F32)


def dot_three(stacked, high, low):
    half = stacked.shape[0] // 2
    both = dot(stacked, high)
    return both[:half] + both[half:] + dot(stacked[:half], low)


def apply_wide(beside, value):
    high, low = split(value)
    depth = beside.shape[1] // 2
    return dot(beside, jnp.concatenate([high, high], axis=0)) + dot(beside[:, :depth], low)


def exact(left, right, contract):
    return lax.dot_general(
        left, right, (contract, ((), ())), precision=lax.Precision.HIGHEST,
        preferred_element_type=F32,
    )


def lane_group(shape, width):
    return lax.broadcasted_iota(jnp.int32, shape, len(shape) - 1) // width


def spread(value, group, width):
    kept = jnp.where(lane_group(value.shape, width) == group, value, 0.0)
    return fold(kept, width)


def fold(value, width):
    lanes = value.shape[-1]
    groups = lanes // width
    if groups & (groups - 1) == 0:
        step = lanes // 2
        while step >= width:
            value = value + pltpu.roll(value, step, value.ndim - 1)
            step //= 2
        return value
    total = value
    for k in range(1, groups):
        total = total + pltpu.roll(value, k * width, value.ndim - 1)
    return total


def column_of(row):
    n = row.shape[1]
    shape = (n, n)
    diagonal = lax.broadcasted_iota(jnp.int32, shape, 0) == lax.broadcasted_iota(jnp.int32, shape, 1)
    return jnp.sum(jnp.where(diagonal, jnp.broadcast_to(row, shape), 0.0), axis=1, keepdims=True)


def lane_table(values, shape, width):
    groups = lane_group(shape, width)
    out = jnp.full(shape, float(values[0]), F32)
    for j in range(1, len(values)):
        out = jnp.where(groups == j, float(values[j]), out)
    return out


def call(kernel, out_shape, in_specs, scratch=(), micros=1.0, limit=VMEM_LIMIT):
    single = not isinstance(out_shape, (tuple, list))
    return pl.pallas_call(
        kernel,
        out_shape=out_shape,
        in_specs=in_specs,
        out_specs=VMEM() if single else [VMEM()] * len(out_shape),
        scratch_shapes=list(scratch),
        compiler_params=pltpu.CompilerParams(vmem_limit_bytes=limit),
        cost_estimate=pl.CostEstimate(flops=int(micros * FLOPS_PER_MICRO), bytes_accessed=0, transcendentals=0),
    )


VMEM = functools.partial(pl.BlockSpec, memory_space=pltpu.VMEM)
SMEM = functools.partial(pl.BlockSpec, memory_space=pltpu.SMEM)
HBM = functools.partial(pl.BlockSpec, memory_space=pltpu.HBM)


def per_device(neighbours, couplings, eigvectors, eigvalues, start_block):
    blk_dev, blk = eigvalues.shape
    nnb = neighbours.shape[1]
    ncol = start_block.shape[1]
    rows_here = blk_dev * blk
    count = lax.axis_size("shift")
    nrows = lax.axis_size("rows")
    total = rows_here * nrows
    width = ncol // count
    packs = blk_dev // count
    wide = 2 * ncol
    here = lax.axis_index("shift")
    me = lax.axis_index("rows")
    paired = nrows % 2 == 0
    halves = 2 if count % 2 == 0 else 1
    per_half = blk_dev // halves
    half_id = here % halves

    angle = np.pi * (np.arange(count, dtype=np.float64) + 0.5) / count
    real_parts = RADIUS * np.cos(angle)
    imag_parts = RADIUS * np.sin(angle)

    def inverse_scale(energy):
        offset = lane_table(real_parts, (1, ncol), width) - energy
        imag = lane_table(imag_parts, (1, ncol), width)
        inverse = 1.0 / (offset * offset + imag * imag)
        return offset * inverse, -(imag * inverse)

    def own_group():
        return lax.axis_index("shift")

    def block_rows(i):
        return slice((i // count) * blk, (i // count + 1) * blk)

    def store_packed(ref, i, value):
        kept = jnp.where(lane_group(value.shape, width) == i % count, value, 0.0)
        if i % count == 0:
            ref[block_rows(i), :] = kept
        else:
            ref[block_rows(i), :] += kept

    def swap(value):
        if paired:
            return lax.ppermute(value, "rows", [(i, i ^ 1) for i in range(nrows)])
        return lax.ppermute(value, "rows", [(i + 1, i) for i in range(nrows - 1)])

    def pass_on(value, arrived):
        if paired:
            pairs = [(i, i + 2) for i in range(0, nrows - 2, 2)] + [(i, i - 2) for i in range(3, nrows, 2)]
            return lax.ppermute(arrived, "rows", pairs)
        return lax.ppermute(value, "rows", [(i, i + 1) for i in range(nrows - 1)])

    def after(value, *others):
        return lax.optimization_barrier((value,) + others)[0]

    def halo(values):
        first = [swap(v) for v in values]
        second = [pass_on(v, a) for v, a in zip(values, first)]
        return first, second

    def mate(value):
        return lax.ppermute(value, "shift", [(i, i ^ 1) for i in range(count)])

    def mate_rows(value, step):
        return jnp.concatenate(
            [value, lax.ppermute(value, "shift", [(i, i ^ step) for i in range(count)])], axis=0
        )

    def rest_of_pairs(value, parts):
        while parts < count:
            value = mate_rows(value, parts)
            parts *= 2
        rows_each = value.shape[0] // count
        return [value[k * rows_each:(k + 1) * rows_each] for k in range(count)]

    def gather_shift(value):
        return [value] + [
            lax.ppermute(value, "shift", [(source(i, k), i) for i in range(count)]) for k in range(1, count)
        ]

    def source(i, k):
        return i ^ k if count & (count - 1) == 0 else (i + count - k) % count

    def sum_rows(value):
        if nrows & (nrows - 1):
            return lax.psum(value, "rows")
        step = 1
        while step < nrows:
            value = value + lax.ppermute(value, "rows", [(i, i ^ step) for i in range(nrows)])
            step *= 2
        return value

    place = neighbours - (me * blk_dev - blk_dev)
    group = place // blk_dev
    partner_group = jnp.where(me % 2 == 0, 2, 0) if paired else 2
    slot = place % blk_dev + blk_dev * jnp.where(group == 1, 0, jnp.where(group == partner_group, 1, 2))
    slot = slot.astype(jnp.int32)

    lead = lax.dynamic_slice_in_dim(eigvectors, half_id * per_half, per_half, axis=0).reshape(per_half * blk, blk)

    def put(xh, xl, block, value):
        rows = pl.ds(pl.multiple_of(block * blk, blk), blk)
        h, l = split(value)
        xh[rows, :] = h
        xl[rows, :] = l

    def prepare(
        start_hbm, vec_hbm, coup_hbm, val, spun, packed, vec_st, vec_ts, cst, start, vec, coup, sems
    ):
        blocks = range(blk_dev)
        copies, late = [], []
        for i in blocks:
            rows = pl.ds(i * blk, blk)
            copies.append(pltpu.make_async_copy(vec_hbm.at[i], vec.at[i], sems.at[i]))
            copies.append(pltpu.make_async_copy(start_hbm.at[rows], start.at[rows], sems.at[blk_dev + i]))
            late.append(pltpu.make_async_copy(coup_hbm.at[i], coup.at[i], sems.at[2 * blk_dev + i]))
        for copy in copies + late:
            copy.start()
        for copy in copies:
            copy.wait()
        mine_now = own_group()
        packed[packs * blk:, :] = val[...]
        backward, rights = [], []
        for i in blocks:
            v = vec[i]
            backward.append(jnp.concatenate(split(v.T), axis=1))
            vec_st[i] = jnp.concatenate(split(v), axis=1)
            vec_ts[i] = backward[i]
            rights.append(spread(start[i * blk:(i + 1) * blk, :], mine_now, width))
        turned = [apply_wide(backward[i], rights[i]) for i in blocks]
        for i in blocks:
            spun[i] = turned[i]
            store_packed(packed, i, turned[i])
        for i in blocks:
            late[i].wait()
            for k in range(nnb):
                ch, cl = split(coup[i, k])
                cst[i, :blk, k * blk:(k + 1) * blk] = ch
                cst[i, blk:, k * blk:(k + 1) * blk] = cl

    sds = jax.ShapeDtypeStruct
    spun, packed, vec_st, vec_ts, cst = call(
        prepare,
        (
            sds((blk_dev, blk, ncol), F32),
            sds((packs * blk + blk_dev, ncol), F32),
            sds((blk_dev, blk, 2 * blk), BF16),
            sds((blk_dev, blk, 2 * blk), BF16),
            sds((blk_dev, 2 * blk, nnb * blk), BF16),
        ),
        in_specs=[HBM()] * 3 + [VMEM()],
        scratch=[
            pltpu.VMEM((rows_here, ncol), F32), pltpu.VMEM((blk_dev, blk, blk), F32),
            pltpu.VMEM((blk_dev, nnb, blk, blk), F32), pltpu.SemaphoreType.DMA((3 * blk_dev,)),
        ],
        micros=20.0, limit=FIRST_LIMIT,
    )(start_block, eigvectors, couplings, eigvalues)

    lead_first = after(swap(lead), packed)
    pack_first = swap(after(packed, lead_first))
    lead_second = pass_on(lead, lead_first)
    pack_second = pass_on(packed, pack_first)

    mate_first = [mate(after(lead_first, pack_first))] if halves == 2 else []

    def fill_first(inputs, xh, xl, offset):
        pack = inputs[0]
        names, lefts, rights = [], [], []
        for h in range(halves):
            base = ((lax.axis_index("shift") + h) % halves) * per_half if halves > 1 else 0
            for j in range(per_half):
                b = base + j
                row0 = pl.multiple_of((b // count) * blk, blk)
                turned = spread(pack[pl.ds(row0, blk), :], b % count, width) * DAMPING
                re, im = inverse_scale(column_of(pack[pl.ds(packs * blk + b, 1), :]))
                vector = inputs[1 + h][j * blk:(j + 1) * blk, :]
                names.append(b)
                lefts.append(jnp.concatenate(split(vector), axis=1))
                rights.append(jnp.concatenate([re * turned, im * turned], axis=1))
        fields = [apply_wide(left, right) for left, right in zip(lefts, rights)]
        for b, field in zip(names, fields):
            put(xh, xl, b + offset, field)

    partners = [pack_first, lead_first] + mate_first

    def first_two(*refs):
        spun_ref, val, vec = refs[:3]
        inputs = refs[3:3 + len(partners)]
        xh, xl, scale = refs[3 + len(partners):]
        firsts = []
        for i in range(blk_dev):
            turned = DAMPING * spun_ref[i]
            re, im = inverse_scale(column_of(val[i:i + 1, :]))
            scale[i, :, :ncol] = re
            scale[i, :, ncol:] = im
            firsts.append(jnp.concatenate([re * turned, im * turned], axis=1))
        fields = [apply_wide(vec[i], firsts[i]) for i in range(blk_dev)]
        for i in range(blk_dev):
            put(xh, xl, i, fields[i])
        fill_first(inputs, xh, xl, blk_dev)

    two_shape = (sds((2 * rows_here, wide), BF16),) * 2 + (sds((blk_dev, blk, wide), F32),)
    two_h, two_l, scale = call(
        first_two, two_shape, in_specs=[VMEM()] * (3 + len(partners)), micros=2.0,
    )(spun, eigvalues, vec_st, *partners)

    def near_of(ref, slots, i):
        return jnp.concatenate(
            [ref[pl.ds(pl.multiple_of(slots[i, k] * blk, blk), blk), :] for k in range(nnb)], axis=0
        )

    def coupled(slots, c, xh, xl, i):
        return dot_three(c[i], near_of(xh, slots, i), near_of(xl, slots, i))

    def times(s, g):
        re, im = g[:, :ncol], g[:, ncol:]
        sre, sim = s[:, :ncol], s[:, ncol:]
        return jnp.concatenate([sre * re - sim * im, sre * im + sim * re], axis=1)

    def plus_real(g, b):
        return jnp.concatenate([g[:, :ncol] + b, g[:, ncol:]], axis=1)

    sizes = [blk_dev // CHUNKS] * CHUNKS if blk_dev % CHUNKS == 0 else [blk_dev]
    chunks = len(sizes)
    spots = [(c, j) for c in range(chunks) for j in range(sizes[c])]

    mate_second = [mate(after(lead_second, pack_second))] if halves == 2 else []
    others = [pack_second, lead_second] + mate_second

    def second_iterate(*refs):
        slots, th, tl, c, vec, vec_t, spun_ref, scale_ref = refs[:8]
        inputs = refs[8:8 + len(others)]
        outs = refs[8 + len(others):8 + len(others) + chunks]
        hats, xh, xl = refs[8 + len(others) + chunks:]
        fill_first(inputs, xh, xl, 2 * blk_dev)
        xh[:2 * rows_here, :] = th[...]
        xl[:2 * rows_here, :] = tl[...]
        blocks = range(blk_dev)
        sums = [coupled(slots, c, xh, xl, i) for i in blocks]
        turned = [apply_wide(vec_t[i], sums[i]) for i in blocks]
        for i in blocks:
            hats[i] = times(scale_ref[i], DAMPING * plus_real(turned[i], (1.0 + KEEP) * spun_ref[i]))
        result = [apply_wide(vec[i], hats[i]) for i in blocks]
        for i in blocks:
            q, j = spots[i]
            outs[q][j] = result[i]

    field_scratch = [pltpu.VMEM((3 * rows_here, wide), BF16)] * 2
    *own, hats = call(
        second_iterate,
        [sds((size, blk, wide), F32) for size in sizes] + [sds((blk_dev, blk, wide), F32)],
        in_specs=[SMEM()] + [VMEM()] * (7 + len(others)),
        scratch=field_scratch,
        micros=6.0,
    )(slot, two_h, two_l, cst, vec_st, vec_ts, spun, scale, *others)

    two_first, two_second = halo(own)

    def third_iterate(*refs):
        slots = refs[0]
        fields = refs[1:1 + 3 * chunks]
        hats_ref, c, vec, vec_t, spun_ref, scale_ref, val = refs[1 + 3 * chunks:8 + 3 * chunks]
        packed_out, diag_out, xh, xl = refs[8 + 3 * chunks:]
        for side in range(3):
            for i, (q, j) in enumerate(spots):
                put(xh, xl, side * blk_dev + i, fields[side * chunks + q][j])
        weight_re = lane_table(real_parts / count, (1, ncol), width)
        weight_im = lane_table(imag_parts / count, (1, ncol), width)
        blocks = range(blk_dev)
        sums = [coupled(slots, c, xh, xl, i) for i in blocks]
        turned = [apply_wide(vec_t[i], sums[i]) for i in blocks]
        ends = []
        for i in blocks:
            hat = KEEP * hats_ref[i] + times(scale_ref[i], DAMPING * plus_real(turned[i], spun_ref[i]))
            term = fold(weight_re * hat[:, :ncol] - weight_im * hat[:, ncol:], width)
            energy = column_of(val[i:i + 1, :])
            ends.append(jnp.concatenate([term, energy * term], axis=1))
        result = [apply_wide(vec[i], ends[i]) for i in blocks]
        for i in blocks:
            diag_out[i] = result[i][:, ncol:]
            store_packed(packed_out, i, result[i][:, :ncol])

    filtered, diagonal = call(
        third_iterate,
        (sds((packs * blk, ncol), F32), sds((blk_dev, blk, ncol), F32)),
        in_specs=[SMEM()] + [VMEM()] * (7 + 3 * chunks),
        scratch=field_scratch,
        micros=6.0,
    )(slot, *own, *two_first, *two_second, hats, cst, vec_st, vec_ts, spun, scale, eigvalues)

    (filt_first,), (filt_second,) = halo([filtered])
    filt_all = gather_shift(filtered)

    def unpacked(refs, rows, g):
        lanes = lane_group((rows.stop - rows.start, ncol), width)
        out = jnp.zeros(lanes.shape, F32)
        mine_now = own_group()
        for k, ref in enumerate(refs):
            s = source(mine_now, k) if k else mine_now
            moved = pltpu.roll(ref[rows, :], ((s - g + count) % count) * width, 1)
            out = jnp.where(lanes == s, moved, out)
        return out

    half_col = ncol // 2

    def triangle(gram):
        top, low = gram[:half_col, :], gram[half_col:, :]
        lanes = lax.broadcasted_iota(jnp.int32, top.shape, 1)
        rows = lax.broadcasted_iota(jnp.int32, top.shape, 0)
        body = jnp.where(lanes - half_col >= rows, low, pltpu.roll(top, half_col, 1))
        diagonal = jnp.sum(jnp.where(lanes == rows, top, 0.0), axis=0, keepdims=True)
        return body, jnp.broadcast_to(diagonal, (8, ncol))

    def whole_of(body, diagonal):
        lanes = lax.broadcasted_iota(jnp.int32, body.shape, 1)
        rows = lax.broadcasted_iota(jnp.int32, body.shape, 0)
        moved = pltpu.roll(body, half_col, 1)
        top = jnp.where((lanes < rows) | (lanes >= half_col), moved, jnp.where(lanes == rows, 0.5 * diagonal, 0.0))
        past = lanes - half_col
        low = jnp.where(past > rows, body, jnp.where(past == rows, 0.5 * body, 0.0))
        both = jnp.concatenate([top, low], axis=0)
        return both + both.T

    def gram_of(*refs):
        pieces, full, gram = refs[:count], refs[count], refs[1 + count]
        for i in range(blk_dev):
            full[i * blk:(i + 1) * blk, :] = unpacked(pieces, block_rows(i), i % count)
        body, diagonal = triangle(exact(full[...], full[...], ((0,), (0,))))
        gram[:half_col, :] = body
        gram[half_col:, :] = diagonal

    full, gram = call(
        gram_of,
        (sds((rows_here, ncol), F32), sds((half_col + 8, ncol), F32)),
        in_specs=[VMEM()] * count,
        micros=GRAM_MICROS,
    )(*filt_all)

    span = ncol // count

    def image_of(slots, own_f, first_f, second_f, full_ref, c, diag, joined, xh, xl, image_ref):
        for f, field in enumerate((own_f, first_f, second_f)):
            for b in range(blk_dev):
                put(xh, xl, f * blk_dev + b, spread(field[block_rows(b), :], b % count, width))
        for i in range(blk_dev):
            image = diag[i] + coupled(slots, c, xh, xl, i)
            image_ref[i * blk:(i + 1) * blk, :] = image
            store_packed(joined, i, image)
        part = exact(full_ref[...], image_ref[...], ((0,), (0,)))
        piece = jnp.zeros((span, ncol), F32)
        for s in range(count):
            piece = piece + jnp.where(
                lane_group((span, ncol), width) == s, part[s * span:(s + 1) * span, :], 0.0
            )
        joined[packs * blk:, :] = piece

    joined = call(
        image_of,
        sds((packs * blk + span, ncol), F32),
        in_specs=[SMEM()] + [VMEM()] * 6,
        scratch=[pltpu.VMEM((3 * rows_here, ncol), BF16)] * 2 + [pltpu.VMEM((rows_here, ncol), F32)],
        micros=3.8,
    )(slot, filtered, filt_first, filt_second, full, cst, diagonal)

    if count & (count - 1):
        pieces, parts = gather_shift(joined), count
    else:
        parts = min(2, count)
        both = mate_rows(joined, 1) if parts == 2 else joined
        pieces = [both[k * (packs * blk + span):(k + 1) * (packs * blk + span)] for k in range(parts)]
    sums = sum_rows(jnp.concatenate([gram] + [piece[packs * blk:] for piece in pieces], axis=0))
    image_all = rest_of_pairs(jnp.concatenate([piece[:packs * blk] for piece in pieces], axis=0), parts)
    moment_all = rest_of_pairs(after(sums[half_col + 8:], *image_all), parts)

    def factor_of(*refs):
        sums_ref, full_ref, pieces = refs[0], refs[1], refs[2:2 + count]
        inverse, basis_ref, image_ref, raw = refs[2 + count:]
        tiles = ncol // 8
        gram_now = whole_of(sums_ref[:half_col, :], sums_ref[half_col:half_col + 1, :]) * (1.0 / total)
        a = [gram_now[t * 8:(t + 1) * 8, :] for t in range(tiles)]
        lanes = lax.broadcasted_iota(jnp.int32, (8, ncol), 1)
        subs = lax.broadcasted_iota(jnp.int32, (8, ncol), 0)
        e = [jnp.where(lanes == subs + t * 8, 1.0, 0.0).astype(F32) for t in range(tiles)]
        for t in range(tiles):
            below = range(t, tiles)
            cols = [
                {u: jnp.broadcast_to(a[u][:, t * 8 + j:t * 8 + j + 1], (8, ncol)) for u in below} for j in range(8)
            ]
            rows = [a[t][j:j + 1, :] for j in range(8)]
            erows = [e[t][j:j + 1, :] for j in range(8)]
            factors = []
            for j in range(8):
                inv = 1.0 / cols[j][t][j:j + 1, :]
                m = {u: cols[j][u] * inv for u in below}
                m[t] = jnp.where(subs > j, m[t], 0.0)
                for q in range(j + 1, 8):
                    above = cols[q][t][j:j + 1, :]
                    for u in below:
                        cols[q][u] = cols[q][u] - m[u] * above
                    left = m[t][q:q + 1, :]
                    rows[q] = rows[q] - left * rows[j]
                    erows[q] = erows[q] - left * erows[j]
                factors.append(m)
            for u in below:
                for j in range(8):
                    a[u] = a[u] - factors[j][u] * rows[j]
                    e[u] = e[u] - factors[j][u] * erows[j]
        for t in range(tiles):
            pivot = jnp.sum(jnp.where(lanes == subs + t * 8, a[t], 0.0), axis=1, keepdims=True)
            inverse[t * 8:(t + 1) * 8, :] = e[t] * (1.0 / jnp.sqrt(pivot))

        inv = inverse[...]
        for i in range(blk_dev):
            raw[i * blk:(i + 1) * blk, :] = unpacked(pieces, block_rows(i), i % count)
        turned = inv.T
        basis_ref[...] = apply_wide(jnp.concatenate(split(full_ref[...]), axis=1), turned)
        image_ref[...] = apply_wide(jnp.concatenate(split(raw[...]), axis=1), turned)

    inverse, basis, basis_image = call(
        factor_of,
        (sds((ncol, ncol), F32), sds((rows_here, ncol), F32), sds((rows_here, ncol), F32)),
        in_specs=[VMEM()] * (2 + count),
        scratch=[pltpu.VMEM((rows_here, ncol), F32)],
        micros=0.5,
    )(sums, full, *image_all)

    def project(*refs):
        moments, inv_ref, projected_ref = refs[:count], refs[count], refs[count + 1]
        inv = inv_ref[...]
        strips = [unpacked(moments, slice(0, span), g) for g in range(count)]
        m = jnp.concatenate(strips, axis=0) * (1.0 / total)
        projected_ref[...] = exact(exact(inv, m, ((1,), (0,))), inv, ((1,), (1,)))

    projected = call(
        project, sds((ncol, ncol), F32), in_specs=[VMEM()] * (count + 1), micros=1.0,
    )(*moment_all, inverse)
    return (basis, basis_image, projected)


def solution(mesh):
    in_specs = (
        P("rows", None),
        P("rows", None, None, None),
        P("rows", None, None),
        P("rows", None),
        P("rows", None),
    )
    out_specs = (P("rows", None), P("rows", None), P())
    return jax.shard_map(
        per_device, mesh=mesh, in_specs=in_specs, out_specs=out_specs, check_vma=False
    )
```

```python
import functools

import jax
import jax.numpy as jnp
import numpy as np
from jax import lax
from jax.experimental import pallas as pl
from jax.experimental.pallas import tpu as pltpu
from jax.sharding import PartitionSpec as P

RADIUS = 1.0
DAMPING = 0.8
CHUNKS = 4
KEEP = 1.0 - DAMPING
VMEM_LIMIT = 24 * 1024 * 1024
FIRST_LIMIT = 52 * 1024 * 1024
FLOPS_PER_MICRO = 1.1e9
GRAM_MICROS = 6.0
F32 = jnp.float32
BF16 = jnp.bfloat16


def split(value):
    high = value.astype(BF16)
    low = (value - high.astype(F32)).astype(BF16)
    return high, low


def dot(left, right):
    return jnp.dot(left, right, preferred_element_type=F32)


def dot_three(stacked, high, low):
    half = stacked.shape[0] // 2
    both = dot(stacked, high)
    return both[:half] + both[half:] + dot(stacked[:half], low)


def apply_wide(beside, value):
    high, low = split(value)
    depth = beside.shape[1] // 2
    return dot(beside, jnp.concatenate([high, high], axis=0)) + dot(beside[:, :depth], low)


def exact(left, right, contract):
    return lax.dot_general(
        left, right, (contract, ((), ())), precision=lax.Precision.HIGHEST,
        preferred_element_type=F32,
    )


def lane_group(shape, width):
    return lax.broadcasted_iota(jnp.int32, shape, len(shape) - 1) // width


def spread(value, group, width):
    kept = jnp.where(lane_group(value.shape, width) == group, value, 0.0)
    return fold(kept, width)


def fold(value, width):
    lanes = value.shape[-1]
    groups = lanes // width
    if groups & (groups - 1) == 0:
        step = lanes // 2
        while step >= width:
            value = value + pltpu.roll(value, step, value.ndim - 1)
            step //= 2
        return value
    total = value
    for k in range(1, groups):
        total = total + pltpu.roll(value, k * width, value.ndim - 1)
    return total


def column_of(row):
    n = row.shape[1]
    shape = (n, n)
    diagonal = lax.broadcasted_iota(jnp.int32, shape, 0) == lax.broadcasted_iota(jnp.int32, shape, 1)
    return jnp.sum(jnp.where(diagonal, jnp.broadcast_to(row, shape), 0.0), axis=1, keepdims=True)


def lane_table(values, shape, width):
    groups = lane_group(shape, width)
    out = jnp.full(shape, float(values[0]), F32)
    for j in range(1, len(values)):
        out = jnp.where(groups == j, float(values[j]), out)
    return out


def call(kernel, out_shape, in_specs, scratch=(), micros=1.0, limit=VMEM_LIMIT):
    single = not isinstance(out_shape, (tuple, list))
    return pl.pallas_call(
        kernel,
        out_shape=out_shape,
        in_specs=in_specs,
        out_specs=VMEM() if single else [VMEM()] * len(out_shape),
        scratch_shapes=list(scratch),
        compiler_params=pltpu.CompilerParams(vmem_limit_bytes=limit),
        cost_estimate=pl.CostEstimate(flops=int(micros * FLOPS_PER_MICRO), bytes_accessed=0, transcendentals=0),
    )


VMEM = functools.partial(pl.BlockSpec, memory_space=pltpu.VMEM)
SMEM = functools.partial(pl.BlockSpec, memory_space=pltpu.SMEM)
HBM = functools.partial(pl.BlockSpec, memory_space=pltpu.HBM)


def per_device(neighbours, couplings, eigvectors, eigvalues, start_block):
    blk_dev, blk = eigvalues.shape
    nnb = neighbours.shape[1]
    ncol = start_block.shape[1]
    rows_here = blk_dev * blk
    count = lax.axis_size("shift")
    nrows = lax.axis_size("rows")
    total = rows_here * nrows
    width = ncol // count
    packs = blk_dev // count
    wide = 2 * ncol
    here = lax.axis_index("shift")
    me = lax.axis_index("rows")
    paired = nrows % 2 == 0
    halves = 2 if count % 2 == 0 else 1
    per_half = blk_dev // halves
    half_id = here % halves

    angle = np.pi * (np.arange(count, dtype=np.float64) + 0.5) / count
    real_parts = RADIUS * np.cos(angle)
    imag_parts = RADIUS * np.sin(angle)

    def inverse_scale(energy):
        offset = lane_table(real_parts, (1, ncol), width) - energy
        imag = lane_table(imag_parts, (1, ncol), width)
        inverse = 1.0 / (offset * offset + imag * imag)
        return offset * inverse, -(imag * inverse)

    def own_group():
        return lax.axis_index("shift")

    def block_rows(i):
        return slice((i // count) * blk, (i // count + 1) * blk)

    def store_packed(ref, i, value):
        kept = jnp.where(lane_group(value.shape, width) == i % count, value, 0.0)
        if i % count == 0:
            ref[block_rows(i), :] = kept
        else:
            ref[block_rows(i), :] += kept

    def swap(value):
        if paired:
            return lax.ppermute(value, "rows", [(i, i ^ 1) for i in range(nrows)])
        return lax.ppermute(value, "rows", [(i + 1, i) for i in range(nrows - 1)])

    def pass_on(value, arrived):
        if paired:
            pairs = [(i, i + 2) for i in range(0, nrows - 2, 2)] + [(i, i - 2) for i in range(3, nrows, 2)]
            return lax.ppermute(arrived, "rows", pairs)
        return lax.ppermute(value, "rows", [(i, i + 1) for i in range(nrows - 1)])

    def after(value, *others):
        return lax.optimization_barrier((value,) + others)[0]

    def halo(values):
        first = [swap(v) for v in values]
        second = [pass_on(v, a) for v, a in zip(values, first)]
        return first, second

    def mate(value):
        return lax.ppermute(value, "shift", [(i, i ^ 1) for i in range(count)])

    def mate_rows(value, step):
        return jnp.concatenate(
            [value, lax.ppermute(value, "shift", [(i, i ^ step) for i in range(count)])], axis=0
        )

    def rest_of_pairs(value, parts):
        while parts < count:
            value = mate_rows(value, parts)
            parts *= 2
        rows_each = value.shape[0] // count
        return [value[k * rows_each:(k + 1) * rows_each] for k in range(count)]

    def gather_shift(value):
        return [value] + [
            lax.ppermute(value, "shift", [(source(i, k), i) for i in range(count)]) for k in range(1, count)
        ]

    def source(i, k):
        return i ^ k if count & (count - 1) == 0 else (i + count - k) % count

    def sum_rows(value):
        if nrows & (nrows - 1):
            return lax.psum(value, "rows")
        step = 1
        while step < nrows:
            value = value + lax.ppermute(value, "rows", [(i, i ^ step) for i in range(nrows)])
            step *= 2
        return value

    place = neighbours - (me * blk_dev - blk_dev)
    group = place // blk_dev
    partner_group = jnp.where(me % 2 == 0, 2, 0) if paired else 2
    slot = place % blk_dev + blk_dev * jnp.where(group == 1, 0, jnp.where(group == partner_group, 1, 2))
    slot = slot.astype(jnp.int32)

    lead = lax.dynamic_slice_in_dim(eigvectors, half_id * per_half, per_half, axis=0).reshape(per_half * blk, blk)

    def put(xh, xl, block, value):
        rows = pl.ds(pl.multiple_of(block * blk, blk), blk)
        h, l = split(value)
        xh[rows, :] = h
        xl[rows, :] = l

    def prepare(
        start_hbm, vec_hbm, coup_hbm, val, spun, packed, vec_st, vec_ts, cst, start, vec, coup, sems
    ):
        blocks = range(blk_dev)
        copies, late = [], []
        for i in blocks:
            rows = pl.ds(i * blk, blk)
            copies.append(pltpu.make_async_copy(vec_hbm.at[i], vec.at[i], sems.at[i]))
            copies.append(pltpu.make_async_copy(start_hbm.at[rows], start.at[rows], sems.at[blk_dev + i]))
            late.append(pltpu.make_async_copy(coup_hbm.at[i], coup.at[i], sems.at[2 * blk_dev + i]))
        for copy in copies + late:
            copy.start()
        for copy in copies:
            copy.wait()
        mine_now = own_group()
        packed[packs * blk:, :] = val[...]
        backward, rights = [], []
        for i in blocks:
            v = vec[i]
            backward.append(jnp.concatenate(split(v.T), axis=1))
            vec_st[i] = jnp.concatenate(split(v), axis=1)
            vec_ts[i] = backward[i]
            rights.append(spread(start[i * blk:(i + 1) * blk, :], mine_now, width))
        turned = [apply_wide(backward[i], rights[i]) for i in blocks]
        for i in blocks:
            spun[i] = turned[i]
            store_packed(packed, i, turned[i])
        for i in blocks:
            late[i].wait()
            for k in range(nnb):
                ch, cl = split(coup[i, k])
                cst[i, :blk, k * blk:(k + 1) * blk] = ch
                cst[i, blk:, k * blk:(k + 1) * blk] = cl

    sds = jax.ShapeDtypeStruct
    spun, packed, vec_st, vec_ts, cst = call(
        prepare,
        (
            sds((blk_dev, blk, ncol), F32),
            sds((packs * blk + blk_dev, ncol), F32),
            sds((blk_dev, blk, 2 * blk), BF16),
            sds((blk_dev, blk, 2 * blk), BF16),
            sds((blk_dev, 2 * blk, nnb * blk), BF16),
        ),
        in_specs=[HBM()] * 3 + [VMEM()],
        scratch=[
            pltpu.VMEM((rows_here, ncol), F32), pltpu.VMEM((blk_dev, blk, blk), F32),
            pltpu.VMEM((blk_dev, nnb, blk, blk), F32), pltpu.SemaphoreType.DMA((3 * blk_dev,)),
        ],
        micros=20.0, limit=FIRST_LIMIT,
    )(start_block, eigvectors, couplings, eigvalues)

    lead_first = after(swap(lead), packed)
    pack_first = swap(after(packed, lead_first))
    lead_second = pass_on(lead, lead_first)
    pack_second = pass_on(packed, pack_first)

    mate_first = [mate(after(lead_first, pack_first))] if halves == 2 else []

    def fill_first(inputs, xh, xl, offset):
        pack = inputs[0]
        names, lefts, rights = [], [], []
        for h in range(halves):
            base = ((lax.axis_index("shift") + h) % halves) * per_half if halves > 1 else 0
            for j in range(per_half):
                b = base + j
                row0 = pl.multiple_of((b // count) * blk, blk)
                turned = spread(pack[pl.ds(row0, blk), :], b % count, width) * DAMPING
                re, im = inverse_scale(column_of(pack[pl.ds(packs * blk + b, 1), :]))
                vector = inputs[1 + h][j * blk:(j + 1) * blk, :]
                names.append(b)
                lefts.append(jnp.concatenate(split(vector), axis=1))
                rights.append(jnp.concatenate([re * turned, im * turned], axis=1))
        fields = [apply_wide(left, right) for left, right in zip(lefts, rights)]
        for b, field in zip(names, fields):
            put(xh, xl, b + offset, field)

    partners = [pack_first, lead_first] + mate_first

    def first_two(*refs):
        spun_ref, val, vec = refs[:3]
        inputs = refs[3:3 + len(partners)]
        xh, xl, scale = refs[3 + len(partners):]
        firsts = []
        for i in range(blk_dev):
            turned = DAMPING * spun_ref[i]
            re, im = inverse_scale(column_of(val[i:i + 1, :]))
            scale[i, :, :ncol] = re
            scale[i, :, ncol:] = im
            firsts.append(jnp.concatenate([re * turned, im * turned], axis=1))
        fields = [apply_wide(vec[i], firsts[i]) for i in range(blk_dev)]
        for i in range(blk_dev):
            put(xh, xl, i, fields[i])
        fill_first(inputs, xh, xl, blk_dev)

    two_shape = (sds((2 * rows_here, wide), BF16),) * 2 + (sds((blk_dev, blk, wide), F32),)
    two_h, two_l, scale = call(
        first_two, two_shape, in_specs=[VMEM()] * (3 + len(partners)), micros=2.0,
    )(spun, eigvalues, vec_st, *partners)

    def near_of(ref, slots, i):
        return jnp.concatenate(
            [ref[pl.ds(pl.multiple_of(slots[i, k] * blk, blk), blk), :] for k in range(nnb)], axis=0
        )

    def coupled(slots, c, xh, xl, i):
        return dot_three(c[i], near_of(xh, slots, i), near_of(xl, slots, i))

    def times(s, g):
        re, im = g[:, :ncol], g[:, ncol:]
        sre, sim = s[:, :ncol], s[:, ncol:]
        return jnp.concatenate([sre * re - sim * im, sre * im + sim * re], axis=1)

    def plus_real(g, b):
        return jnp.concatenate([g[:, :ncol] + b, g[:, ncol:]], axis=1)

    sizes = [blk_dev // CHUNKS] * CHUNKS if blk_dev % CHUNKS == 0 else [blk_dev]
    chunks = len(sizes)
    spots = [(c, j) for c in range(chunks) for j in range(sizes[c])]

    mate_second = [mate(after(lead_second, pack_second))] if halves == 2 else []
    others = [pack_second, lead_second] + mate_second

    def second_iterate(*refs):
        slots, th, tl, c, vec, vec_t, spun_ref, scale_ref = refs[:8]
        inputs = refs[8:8 + len(others)]
        outs = refs[8 + len(others):8 + len(others) + chunks]
        hats, xh, xl = refs[8 + len(others) + chunks:]
        fill_first(inputs, xh, xl, 2 * blk_dev)
        xh[:2 * rows_here, :] = th[...]
        xl[:2 * rows_here, :] = tl[...]
        blocks = range(blk_dev)
        sums = [coupled(slots, c, xh, xl, i) for i in blocks]
        turned = [apply_wide(vec_t[i], sums[i]) for i in blocks]
        for i in blocks:
            hats[i] = times(scale_ref[i], DAMPING * plus_real(turned[i], (1.0 + KEEP) * spun_ref[i]))
        result = [apply_wide(vec[i], hats[i]) for i in blocks]
        for i in blocks:
            q, j = spots[i]
            outs[q][j] = result[i]

    field_scratch = [pltpu.VMEM((3 * rows_here, wide), BF16)] * 2
    *own, hats = call(
        second_iterate,
        [sds((size, blk, wide), F32) for size in sizes] + [sds((blk_dev, blk, wide), F32)],
        in_specs=[SMEM()] + [VMEM()] * (7 + len(others)),
        scratch=field_scratch,
        micros=6.0,
    )(slot, two_h, two_l, cst, vec_st, vec_ts, spun, scale, *others)

    two_first, two_second = halo(own)

    def third_iterate(*refs):
        slots = refs[0]
        fields = refs[1:1 + 3 * chunks]
        hats_ref, c, vec, vec_t, spun_ref, scale_ref, val = refs[1 + 3 * chunks:8 + 3 * chunks]
        packed_out, diag_out, xh, xl = refs[8 + 3 * chunks:]
        for side in range(3):
            for i, (q, j) in enumerate(spots):
                put(xh, xl, side * blk_dev + i, fields[side * chunks + q][j])
        weight_re = lane_table(real_parts / count, (1, ncol), width)
        weight_im = lane_table(imag_parts / count, (1, ncol), width)
        blocks = range(blk_dev)
        sums = [coupled(slots, c, xh, xl, i) for i in blocks]
        turned = [apply_wide(vec_t[i], sums[i]) for i in blocks]
        ends = []
        for i in blocks:
            hat = KEEP * hats_ref[i] + times(scale_ref[i], DAMPING * plus_real(turned[i], spun_ref[i]))
            term = fold(weight_re * hat[:, :ncol] - weight_im * hat[:, ncol:], width)
            energy = column_of(val[i:i + 1, :])
            ends.append(jnp.concatenate([term, energy * term], axis=1))
        result = [apply_wide(vec[i], ends[i]) for i in blocks]
        for i in blocks:
            diag_out[i] = result[i][:, ncol:]
            store_packed(packed_out, i, result[i][:, :ncol])

    filtered, diagonal = call(
        third_iterate,
        (sds((packs * blk, ncol), F32), sds((blk_dev, blk, ncol), F32)),
        in_specs=[SMEM()] + [VMEM()] * (7 + 3 * chunks),
        scratch=field_scratch,
        micros=6.0,
    )(slot, *own, *two_first, *two_second, hats, cst, vec_st, vec_ts, spun, scale, eigvalues)

    (filt_first,), (filt_second,) = halo([filtered])
    filt_all = gather_shift(filtered)

    def unpacked(refs, rows, g):
        lanes = lane_group((rows.stop - rows.start, ncol), width)
        out = jnp.zeros(lanes.shape, F32)
        mine_now = own_group()
        for k, ref in enumerate(refs):
            s = source(mine_now, k) if k else mine_now
            moved = pltpu.roll(ref[rows, :], ((s - g + count) % count) * width, 1)
            out = jnp.where(lanes == s, moved, out)
        return out

    half_col = ncol // 2

    def triangle(gram):
        top, low = gram[:half_col, :], gram[half_col:, :]
        lanes = lax.broadcasted_iota(jnp.int32, top.shape, 1)
        rows = lax.broadcasted_iota(jnp.int32, top.shape, 0)
        body = jnp.where(lanes - half_col >= rows, low, pltpu.roll(top, half_col, 1))
        diagonal = jnp.sum(jnp.where(lanes == rows, top, 0.0), axis=0, keepdims=True)
        return body, jnp.broadcast_to(diagonal, (8, ncol))

    def whole_of(body, diagonal):
        lanes = lax.broadcasted_iota(jnp.int32, body.shape, 1)
        rows = lax.broadcasted_iota(jnp.int32, body.shape, 0)
        moved = pltpu.roll(body, half_col, 1)
        top = jnp.where((lanes < rows) | (lanes >= half_col), moved, jnp.where(lanes == rows, 0.5 * diagonal, 0.0))
        past = lanes - half_col
        low = jnp.where(past > rows, body, jnp.where(past == rows, 0.5 * body, 0.0))
        both = jnp.concatenate([top, low], axis=0)
        return both + both.T

    def gram_of(*refs):
        pieces, full, gram = refs[:count], refs[count], refs[1 + count]
        for i in range(blk_dev):
            full[i * blk:(i + 1) * blk, :] = unpacked(pieces, block_rows(i), i % count)
        body, diagonal = triangle(exact(full[...], full[...], ((0,), (0,))))
        gram[:half_col, :] = body
        gram[half_col:, :] = diagonal

    full, gram = call(
        gram_of,
        (sds((rows_here, ncol), F32), sds((half_col + 8, ncol), F32)),
        in_specs=[VMEM()] * count,
        micros=GRAM_MICROS,
    )(*filt_all)

    span = ncol // count

    def image_of(slots, own_f, first_f, second_f, full_ref, c, diag, joined, xh, xl, image_ref):
        for f, field in enumerate((own_f, first_f, second_f)):
            for b in range(blk_dev):
                put(xh, xl, f * blk_dev + b, spread(field[block_rows(b), :], b % count, width))
        for i in range(blk_dev):
            image = diag[i] + coupled(slots, c, xh, xl, i)
            image_ref[i * blk:(i + 1) * blk, :] = image
            store_packed(joined, i, image)
        part = exact(full_ref[...], image_ref[...], ((0,), (0,)))
        piece = jnp.zeros((span, ncol), F32)
        for s in range(count):
            piece = piece + jnp.where(
                lane_group((span, ncol), width) == s, part[s * span:(s + 1) * span, :], 0.0
            )
        joined[packs * blk:, :] = piece

    joined = call(
        image_of,
        sds((packs * blk + span, ncol), F32),
        in_specs=[SMEM()] + [VMEM()] * 6,
        scratch=[pltpu.VMEM((3 * rows_here, ncol), BF16)] * 2 + [pltpu.VMEM((rows_here, ncol), F32)],
        micros=3.8,
    )(slot, filtered, filt_first, filt_second, full, cst, diagonal)

    if count & (count - 1):
        pieces, parts = gather_shift(joined), count
    else:
        parts = min(2, count)
        both = mate_rows(joined, 1) if parts == 2 else joined
        pieces = [both[k * (packs * blk + span):(k + 1) * (packs * blk + span)] for k in range(parts)]
    sums = sum_rows(jnp.concatenate([gram] + [piece[packs * blk:] for piece in pieces], axis=0))
    image_all = rest_of_pairs(jnp.concatenate([piece[:packs * blk] for piece in pieces], axis=0), parts)
    moment_all = rest_of_pairs(after(sums[half_col + 8:], *image_all), parts)

    def factor_of(sums_ref, inverse):
        tiles = ncol // 8
        gram_now = whole_of(sums_ref[:half_col, :], sums_ref[half_col:half_col + 1, :]) * (1.0 / total)
        a = [gram_now[t * 8:(t + 1) * 8, :] for t in range(tiles)]
        lanes = lax.broadcasted_iota(jnp.int32, (8, ncol), 1)
        subs = lax.broadcasted_iota(jnp.int32, (8, ncol), 0)
        e = [jnp.where(lanes == subs + t * 8, 1.0, 0.0).astype(F32) for t in range(tiles)]
        for t in range(tiles):
            below = range(t, tiles)
            cols = [
                {u: jnp.broadcast_to(a[u][:, t * 8 + j:t * 8 + j + 1], (8, ncol)) for u in below} for j in range(8)
            ]
            rows = [a[t][j:j + 1, :] for j in range(8)]
            erows = [e[t][j:j + 1, :] for j in range(8)]
            factors = []
            for j in range(8):
                inv = 1.0 / cols[j][t][j:j + 1, :]
                m = {u: cols[j][u] * inv for u in below}
                m[t] = jnp.where(subs > j, m[t], 0.0)
                for q in range(j + 1, 8):
                    above = cols[q][t][j:j + 1, :]
                    for u in below:
                        cols[q][u] = cols[q][u] - m[u] * above
                    left = m[t][q:q + 1, :]
                    rows[q] = rows[q] - left * rows[j]
                    erows[q] = erows[q] - left * erows[j]
                factors.append(m)
            for u in below:
                for j in range(8):
                    a[u] = a[u] - factors[j][u] * rows[j]
                    e[u] = e[u] - factors[j][u] * erows[j]
        for t in range(tiles):
            pivot = jnp.sum(jnp.where(lanes == subs + t * 8, a[t], 0.0), axis=1, keepdims=True)
            inverse[t * 8:(t + 1) * 8, :] = e[t] * (1.0 / jnp.sqrt(pivot))


    inverse = call(factor_of, sds((ncol, ncol), F32), in_specs=[VMEM()], micros=0.5)(after(sums, *image_all))

    def finish(*refs):
        full_ref, pieces, moments, inv_ref = refs[0], refs[1:1 + count], refs[1 + count:1 + 2 * count], refs[1 + 2 * count]
        basis_ref, image_ref, projected_ref, raw = refs[2 + 2 * count:]
        inv = inv_ref[...]
        turned = inv.T
        strips = [unpacked(moments, slice(0, span), g) for g in range(count)]
        m = jnp.concatenate(strips, axis=0) * (1.0 / total)
        half = exact(inv, m, ((1,), (0,)))
        for i in range(blk_dev):
            raw[i * blk:(i + 1) * blk, :] = unpacked(pieces, block_rows(i), i % count)
        basis_ref[...] = apply_wide(jnp.concatenate(split(full_ref[...]), axis=1), turned)
        image_ref[...] = apply_wide(jnp.concatenate(split(raw[...]), axis=1), turned)
        projected_ref[...] = exact(half, turned, ((1,), (0,)))

    return call(
        finish,
        (sds((rows_here, ncol), F32), sds((rows_here, ncol), F32), sds((ncol, ncol), F32)),
        in_specs=[VMEM()] * (2 + 2 * count),
        scratch=[pltpu.VMEM((rows_here, ncol), F32)],
        micros=3.0,
    )(full, *image_all, *moment_all, inverse)


def solution(mesh):
    in_specs = (
        P("rows", None),
        P("rows", None, None, None),
        P("rows", None, None),
        P("rows", None),
        P("rows", None),
    )
    out_specs = (P("rows", None), P("rows", None), P())
    return jax.shard_map(
        per_device, mesh=mesh, in_specs=in_specs, out_specs=out_specs, check_vma=False
    )
```

```python
import functools

import jax
import jax.numpy as jnp
import numpy as np
from jax import lax
from jax.experimental import pallas as pl
from jax.experimental.pallas import tpu as pltpu
from jax.sharding import PartitionSpec as P

RADIUS = 1.0
DAMPING = 0.8
CHUNKS = 4
KEEP = 1.0 - DAMPING
VMEM_LIMIT = 24 * 1024 * 1024
FIRST_LIMIT = 52 * 1024 * 1024
FLOPS_PER_MICRO = 1.1e9
GRAM_MICROS = 6.0
F32 = jnp.float32
BF16 = jnp.bfloat16


def split(value):
    high = value.astype(BF16)
    low = (value - high.astype(F32)).astype(BF16)
    return high, low


def dot(left, right):
    return jnp.dot(left, right, preferred_element_type=F32)


def dot_three(stacked, high, low):
    half = stacked.shape[0] // 2
    both = dot(stacked, high)
    return both[:half] + both[half:] + dot(stacked[:half], low)


def apply_wide(beside, value):
    high, low = split(value)
    depth = beside.shape[1] // 2
    return dot(beside, jnp.concatenate([high, high], axis=0)) + dot(beside[:, :depth], low)


def exact(left, right, contract):
    return lax.dot_general(
        left, right, (contract, ((), ())), precision=lax.Precision.HIGHEST,
        preferred_element_type=F32,
    )


def lane_group(shape, width):
    return lax.broadcasted_iota(jnp.int32, shape, len(shape) - 1) // width


def spread(value, group, width):
    kept = jnp.where(lane_group(value.shape, width) == group, value, 0.0)
    return fold(kept, width)


def fold(value, width):
    lanes = value.shape[-1]
    groups = lanes // width
    if groups & (groups - 1) == 0:
        step = lanes // 2
        while step >= width:
            value = value + pltpu.roll(value, step, value.ndim - 1)
            step //= 2
        return value
    total = value
    for k in range(1, groups):
        total = total + pltpu.roll(value, k * width, value.ndim - 1)
    return total


def column_of(row):
    n = row.shape[1]
    shape = (n, n)
    diagonal = lax.broadcasted_iota(jnp.int32, shape, 0) == lax.broadcasted_iota(jnp.int32, shape, 1)
    return jnp.sum(jnp.where(diagonal, jnp.broadcast_to(row, shape), 0.0), axis=1, keepdims=True)


def lane_table(values, shape, width):
    groups = lane_group(shape, width)
    out = jnp.full(shape, float(values[0]), F32)
    for j in range(1, len(values)):
        out = jnp.where(groups == j, float(values[j]), out)
    return out


def call(kernel, out_shape, in_specs, scratch=(), micros=1.0, limit=VMEM_LIMIT):
    single = not isinstance(out_shape, (tuple, list))
    return pl.pallas_call(
        kernel,
        out_shape=out_shape,
        in_specs=in_specs,
        out_specs=VMEM() if single else [VMEM()] * len(out_shape),
        scratch_shapes=list(scratch),
        compiler_params=pltpu.CompilerParams(vmem_limit_bytes=limit),
        cost_estimate=pl.CostEstimate(flops=int(micros * FLOPS_PER_MICRO), bytes_accessed=0, transcendentals=0),
    )


VMEM = functools.partial(pl.BlockSpec, memory_space=pltpu.VMEM)
SMEM = functools.partial(pl.BlockSpec, memory_space=pltpu.SMEM)
HBM = functools.partial(pl.BlockSpec, memory_space=pltpu.HBM)


def per_device(neighbours, couplings, eigvectors, eigvalues, start_block):
    blk_dev, blk = eigvalues.shape
    nnb = neighbours.shape[1]
    ncol = start_block.shape[1]
    rows_here = blk_dev * blk
    count = lax.axis_size("shift")
    nrows = lax.axis_size("rows")
    total = rows_here * nrows
    width = ncol // count
    packs = blk_dev // count
    wide = 2 * ncol
    here = lax.axis_index("shift")
    me = lax.axis_index("rows")
    paired = nrows % 2 == 0
    halves = 2 if count % 2 == 0 else 1
    per_half = blk_dev // halves
    half_id = here % halves

    angle = np.pi * (np.arange(count, dtype=np.float64) + 0.5) / count
    real_parts = RADIUS * np.cos(angle)
    imag_parts = RADIUS * np.sin(angle)

    def inverse_scale(energy):
        offset = lane_table(real_parts, (1, ncol), width) - energy
        imag = lane_table(imag_parts, (1, ncol), width)
        inverse = 1.0 / (offset * offset + imag * imag)
        return offset * inverse, -(imag * inverse)

    def own_group():
        return lax.axis_index("shift")

    def block_rows(i):
        return slice((i // count) * blk, (i // count + 1) * blk)

    def store_packed(ref, i, value):
        kept = jnp.where(lane_group(value.shape, width) == i % count, value, 0.0)
        if i % count == 0:
            ref[block_rows(i), :] = kept
        else:
            ref[block_rows(i), :] += kept

    def swap(value):
        if paired:
            return lax.ppermute(value, "rows", [(i, i ^ 1) for i in range(nrows)])
        return lax.ppermute(value, "rows", [(i + 1, i) for i in range(nrows - 1)])

    def pass_on(value, arrived):
        if paired:
            pairs = [(i, i + 2) for i in range(0, nrows - 2, 2)] + [(i, i - 2) for i in range(3, nrows, 2)]
            return lax.ppermute(arrived, "rows", pairs)
        return lax.ppermute(value, "rows", [(i, i + 1) for i in range(nrows - 1)])

    def after(value, *others):
        return lax.optimization_barrier((value,) + others)[0]

    def halo(values):
        first = [swap(v) for v in values]
        second = [pass_on(v, a) for v, a in zip(values, first)]
        return first, second

    def mate(value):
        return lax.ppermute(value, "shift", [(i, i ^ 1) for i in range(count)])

    def mate_rows(value, step):
        return jnp.concatenate(
            [value, lax.ppermute(value, "shift", [(i, i ^ step) for i in range(count)])], axis=0
        )

    def rest_of_pairs(value, parts):
        while parts < count:
            value = mate_rows(value, parts)
            parts *= 2
        rows_each = value.shape[0] // count
        return [value[k * rows_each:(k + 1) * rows_each] for k in range(count)]

    def gather_shift(value):
        return [value] + [
            lax.ppermute(value, "shift", [(source(i, k), i) for i in range(count)]) for k in range(1, count)
        ]

    def source(i, k):
        return i ^ k if count & (count - 1) == 0 else (i + count - k) % count

    def sum_rows(value):
        if nrows & (nrows - 1):
            return lax.psum(value, "rows")
        step = 1
        while step < nrows:
            value = value + lax.ppermute(value, "rows", [(i, i ^ step) for i in range(nrows)])
            step *= 2
        return value

    place = neighbours - (me * blk_dev - blk_dev)
    group = place // blk_dev
    partner_group = jnp.where(me % 2 == 0, 2, 0) if paired else 2
    slot = place % blk_dev + blk_dev * jnp.where(group == 1, 0, jnp.where(group == partner_group, 1, 2))
    slot = slot.astype(jnp.int32)

    lead = lax.dynamic_slice_in_dim(eigvectors, half_id * per_half, per_half, axis=0).reshape(per_half * blk, blk)

    def put(xh, xl, block, value):
        rows = pl.ds(pl.multiple_of(block * blk, blk), blk)
        h, l = split(value)
        xh[rows, :] = h
        xl[rows, :] = l

    def prepare(
        start_hbm, vec_hbm, coup_hbm, val, spun, packed, vec_st, vec_ts, cst, start, vec, coup, sems
    ):
        blocks = range(blk_dev)
        copies, late = [], []
        for i in blocks:
            rows = pl.ds(i * blk, blk)
            copies.append(pltpu.make_async_copy(vec_hbm.at[i], vec.at[i], sems.at[i]))
            copies.append(pltpu.make_async_copy(start_hbm.at[rows], start.at[rows], sems.at[blk_dev + i]))
            late.append(pltpu.make_async_copy(coup_hbm.at[i], coup.at[i], sems.at[2 * blk_dev + i]))
        for copy in copies + late:
            copy.start()
        for copy in copies:
            copy.wait()
        mine_now = own_group()
        packed[packs * blk:, :] = val[...]
        backward, rights = [], []
        for i in blocks:
            v = vec[i]
            backward.append(jnp.concatenate(split(v.T), axis=1))
            vec_st[i] = jnp.concatenate(split(v), axis=1)
            vec_ts[i] = backward[i]
            rights.append(spread(start[i * blk:(i + 1) * blk, :], mine_now, width))
        turned = [apply_wide(backward[i], rights[i]) for i in blocks]
        for i in blocks:
            spun[i] = turned[i]
            store_packed(packed, i, turned[i])
        for i in blocks:
            late[i].wait()
            for k in range(nnb):
                ch, cl = split(coup[i, k])
                cst[i, :blk, k * blk:(k + 1) * blk] = ch
                cst[i, blk:, k * blk:(k + 1) * blk] = cl

    sds = jax.ShapeDtypeStruct
    spun, packed, vec_st, vec_ts, cst = call(
        prepare,
        (
            sds((blk_dev, blk, ncol), F32),
            sds((packs * blk + blk_dev, ncol), F32),
            sds((blk_dev, blk, 2 * blk), BF16),
            sds((blk_dev, blk, 2 * blk), BF16),
            sds((blk_dev, 2 * blk, nnb * blk), BF16),
        ),
        in_specs=[HBM()] * 3 + [VMEM()],
        scratch=[
            pltpu.VMEM((rows_here, ncol), F32), pltpu.VMEM((blk_dev, blk, blk), F32),
            pltpu.VMEM((blk_dev, nnb, blk, blk), F32), pltpu.SemaphoreType.DMA((3 * blk_dev,)),
        ],
        micros=20.0, limit=FIRST_LIMIT,
    )(start_block, eigvectors, couplings, eigvalues)

    lead_first = after(swap(lead), packed)
    pack_first = swap(after(packed, lead_first))
    lead_second = pass_on(lead, lead_first)
    pack_second = pass_on(packed, pack_first)

    mate_first = [mate(after(lead_first, pack_first))] if halves == 2 else []

    def fill_first(inputs, xh, xl, offset):
        pack = inputs[0]
        names, lefts, rights = [], [], []
        for h in range(halves):
            base = ((lax.axis_index("shift") + h) % halves) * per_half if halves > 1 else 0
            for j in range(per_half):
                b = base + j
                row0 = pl.multiple_of((b // count) * blk, blk)
                turned = spread(pack[pl.ds(row0, blk), :], b % count, width) * DAMPING
                re, im = inverse_scale(column_of(pack[pl.ds(packs * blk + b, 1), :]))
                vector = inputs[1 + h][j * blk:(j + 1) * blk, :]
                names.append(b)
                lefts.append(jnp.concatenate(split(vector), axis=1))
                rights.append(jnp.concatenate([re * turned, im * turned], axis=1))
        fields = [apply_wide(left, right) for left, right in zip(lefts, rights)]
        for b, field in zip(names, fields):
            put(xh, xl, b + offset, field)

    partners = [pack_first, lead_first] + mate_first

    def first_two(*refs):
        spun_ref, val, vec = refs[:3]
        inputs = refs[3:3 + len(partners)]
        xh, xl, scale = refs[3 + len(partners):]
        firsts = []
        for i in range(blk_dev):
            turned = DAMPING * spun_ref[i]
            re, im = inverse_scale(column_of(val[i:i + 1, :]))
            scale[i, :, :ncol] = re
            scale[i, :, ncol:] = im
            firsts.append(jnp.concatenate([re * turned, im * turned], axis=1))
        fields = [apply_wide(vec[i], firsts[i]) for i in range(blk_dev)]
        for i in range(blk_dev):
            put(xh, xl, i, fields[i])
        fill_first(inputs, xh, xl, blk_dev)

    two_shape = (sds((2 * rows_here, wide), BF16),) * 2 + (sds((blk_dev, blk, wide), F32),)
    two_h, two_l, scale = call(
        first_two, two_shape, in_specs=[VMEM()] * (3 + len(partners)), micros=2.0,
    )(spun, eigvalues, vec_st, *partners)

    def near_of(ref, slots, i):
        return jnp.concatenate(
            [ref[pl.ds(pl.multiple_of(slots[i, k] * blk, blk), blk), :] for k in range(nnb)], axis=0
        )

    def coupled(slots, c, xh, xl, i):
        return dot_three(c[i], near_of(xh, slots, i), near_of(xl, slots, i))

    def times(s, g):
        re, im = g[:, :ncol], g[:, ncol:]
        sre, sim = s[:, :ncol], s[:, ncol:]
        return jnp.concatenate([sre * re - sim * im, sre * im + sim * re], axis=1)

    def plus_real(g, b):
        return jnp.concatenate([g[:, :ncol] + b, g[:, ncol:]], axis=1)

    sizes = [blk_dev // CHUNKS] * CHUNKS if blk_dev % CHUNKS == 0 else [blk_dev]
    chunks = len(sizes)
    spots = [(c, j) for c in range(chunks) for j in range(sizes[c])]

    mate_second = [mate(after(lead_second, pack_second))] if halves == 2 else []
    others = [pack_second, lead_second] + mate_second

    def second_iterate(*refs):
        slots, th, tl, c, vec, vec_t, spun_ref, scale_ref = refs[:8]
        inputs = refs[8:8 + len(others)]
        outs = refs[8 + len(others):8 + len(others) + chunks]
        hats, xh, xl = refs[8 + len(others) + chunks:]
        fill_first(inputs, xh, xl, 2 * blk_dev)
        xh[:2 * rows_here, :] = th[...]
        xl[:2 * rows_here, :] = tl[...]
        blocks = range(blk_dev)
        sums = [coupled(slots, c, xh, xl, i) for i in blocks]
        turned = [apply_wide(vec_t[i], sums[i]) for i in blocks]
        for i in blocks:
            hats[i] = times(scale_ref[i], DAMPING * plus_real(turned[i], (1.0 + KEEP) * spun_ref[i]))
        result = [apply_wide(vec[i], hats[i]) for i in blocks]
        for i in blocks:
            q, j = spots[i]
            outs[q][j] = result[i]

    field_scratch = [pltpu.VMEM((3 * rows_here, wide), BF16)] * 2
    *own, hats = call(
        second_iterate,
        [sds((size, blk, wide), F32) for size in sizes] + [sds((blk_dev, blk, wide), F32)],
        in_specs=[SMEM()] + [VMEM()] * (7 + len(others)),
        scratch=field_scratch,
        micros=6.0,
    )(slot, two_h, two_l, cst, vec_st, vec_ts, spun, scale, *others)

    two_first, two_second = halo(own)

    def third_iterate(*refs):
        slots = refs[0]
        fields = refs[1:1 + 3 * chunks]
        hats_ref, c, vec, vec_t, spun_ref, scale_ref, val = refs[1 + 3 * chunks:8 + 3 * chunks]
        packed_out, diag_out, xh, xl = refs[8 + 3 * chunks:]
        for side in range(3):
            for i, (q, j) in enumerate(spots):
                put(xh, xl, side * blk_dev + i, fields[side * chunks + q][j])
        weight_re = lane_table(real_parts / count, (1, ncol), width)
        weight_im = lane_table(imag_parts / count, (1, ncol), width)
        blocks = range(blk_dev)
        sums = [coupled(slots, c, xh, xl, i) for i in blocks]
        turned = [apply_wide(vec_t[i], sums[i]) for i in blocks]
        ends = []
        for i in blocks:
            hat = KEEP * hats_ref[i] + times(scale_ref[i], DAMPING * plus_real(turned[i], spun_ref[i]))
            term = fold(weight_re * hat[:, :ncol] - weight_im * hat[:, ncol:], width)
            energy = column_of(val[i:i + 1, :])
            ends.append(jnp.concatenate([term, energy * term], axis=1))
        result = [apply_wide(vec[i], ends[i]) for i in blocks]
        for i in blocks:
            diag_out[i] = result[i][:, ncol:]
            store_packed(packed_out, i, result[i][:, :ncol])

    filtered, diagonal = call(
        third_iterate,
        (sds((packs * blk, ncol), F32), sds((blk_dev, blk, ncol), F32)),
        in_specs=[SMEM()] + [VMEM()] * (7 + 3 * chunks),
        scratch=field_scratch,
        micros=6.0,
    )(slot, *own, *two_first, *two_second, hats, cst, vec_st, vec_ts, spun, scale, eigvalues)

    (filt_first,), (filt_second,) = halo([filtered])
    filt_all = gather_shift(filtered)

    def unpacked(refs, rows, g):
        lanes = lane_group((rows.stop - rows.start, ncol), width)
        out = jnp.zeros(lanes.shape, F32)
        mine_now = own_group()
        for k, ref in enumerate(refs):
            s = source(mine_now, k) if k else mine_now
            moved = pltpu.roll(ref[rows, :], ((s - g + count) % count) * width, 1)
            out = jnp.where(lanes == s, moved, out)
        return out

    half_col = ncol // 2

    def triangle(gram):
        top, low = gram[:half_col, :], gram[half_col:, :]
        lanes = lax.broadcasted_iota(jnp.int32, top.shape, 1)
        rows = lax.broadcasted_iota(jnp.int32, top.shape, 0)
        body = jnp.where(lanes - half_col >= rows, low, pltpu.roll(top, half_col, 1))
        diagonal = jnp.sum(jnp.where(lanes == rows, top, 0.0), axis=0, keepdims=True)
        return body, jnp.broadcast_to(diagonal, (8, ncol))

    def whole_of(body, diagonal):
        lanes = lax.broadcasted_iota(jnp.int32, body.shape, 1)
        rows = lax.broadcasted_iota(jnp.int32, body.shape, 0)
        moved = pltpu.roll(body, half_col, 1)
        top = jnp.where((lanes < rows) | (lanes >= half_col), moved, jnp.where(lanes == rows, 0.5 * diagonal, 0.0))
        past = lanes - half_col
        low = jnp.where(past > rows, body, jnp.where(past == rows, 0.5 * body, 0.0))
        both = jnp.concatenate([top, low], axis=0)
        return both + both.T

    def gram_of(*refs):
        pieces, full, gram = refs[:count], refs[count], refs[1 + count]
        for i in range(blk_dev):
            full[i * blk:(i + 1) * blk, :] = unpacked(pieces, block_rows(i), i % count)
        body, diagonal = triangle(exact(full[...], full[...], ((0,), (0,))))
        gram[:half_col, :] = body
        gram[half_col:, :] = diagonal

    full, gram = call(
        gram_of,
        (sds((rows_here, ncol), F32), sds((half_col + 8, ncol), F32)),
        in_specs=[VMEM()] * count,
        micros=GRAM_MICROS,
    )(*filt_all)

    span = ncol // count

    def image_of(slots, own_f, first_f, second_f, full_ref, c, diag, joined, xh, xl, image_ref):
        for f, field in enumerate((own_f, first_f, second_f)):
            for b in range(blk_dev):
                put(xh, xl, f * blk_dev + b, spread(field[block_rows(b), :], b % count, width))
        for i in range(blk_dev):
            image = diag[i] + coupled(slots, c, xh, xl, i)
            image_ref[i * blk:(i + 1) * blk, :] = image
            store_packed(joined, i, image)
        left, right = split(full_ref[...]), split(image_ref[...])
        part = sum(
            lax.dot_general(left[a], right[b], (((0,), (0,)), ((), ())), preferred_element_type=F32)
            for a, b in ((0, 0), (0, 1), (1, 0))
        )
        piece = jnp.zeros((span, ncol), F32)
        for s in range(count):
            piece = piece + jnp.where(
                lane_group((span, ncol), width) == s, part[s * span:(s + 1) * span, :], 0.0
            )
        joined[packs * blk:, :] = piece

    joined = call(
        image_of,
        sds((packs * blk + span, ncol), F32),
        in_specs=[SMEM()] + [VMEM()] * 6,
        scratch=[pltpu.VMEM((3 * rows_here, ncol), BF16)] * 2 + [pltpu.VMEM((rows_here, ncol), F32)],
        micros=3.8,
    )(slot, filtered, filt_first, filt_second, full, cst, diagonal)

    if count & (count - 1):
        pieces, parts = gather_shift(joined), count
    else:
        parts = min(2, count)
        both = mate_rows(joined, 1) if parts == 2 else joined
        pieces = [both[k * (packs * blk + span):(k + 1) * (packs * blk + span)] for k in range(parts)]
    sums = sum_rows(jnp.concatenate([gram] + [piece[packs * blk:] for piece in pieces], axis=0))
    image_all = rest_of_pairs(jnp.concatenate([piece[:packs * blk] for piece in pieces], axis=0), parts)
    moment_all = rest_of_pairs(after(sums[half_col + 8:], *image_all), parts)

    def factor_of(sums_ref, inverse):
        tiles = ncol // 8
        gram_now = whole_of(sums_ref[:half_col, :], sums_ref[half_col:half_col + 1, :]) * (1.0 / total)
        a = [gram_now[t * 8:(t + 1) * 8, :] for t in range(tiles)]
        lanes = lax.broadcasted_iota(jnp.int32, (8, ncol), 1)
        subs = lax.broadcasted_iota(jnp.int32, (8, ncol), 0)
        e = [jnp.where(lanes == subs + t * 8, 1.0, 0.0).astype(F32) for t in range(tiles)]
        for t in range(tiles):
            below = range(t, tiles)
            cols = [
                {u: jnp.broadcast_to(a[u][:, t * 8 + j:t * 8 + j + 1], (8, ncol)) for u in below} for j in range(8)
            ]
            rows = [a[t][j:j + 1, :] for j in range(8)]
            erows = [e[t][j:j + 1, :] for j in range(8)]
            factors = []
            for j in range(8):
                inv = 1.0 / cols[j][t][j:j + 1, :]
                m = {u: cols[j][u] * inv for u in below}
                m[t] = jnp.where(subs > j, m[t], 0.0)
                for q in range(j + 1, 8):
                    above = cols[q][t][j:j + 1, :]
                    for u in below:
                        cols[q][u] = cols[q][u] - m[u] * above
                    left = m[t][q:q + 1, :]
                    rows[q] = rows[q] - left * rows[j]
                    erows[q] = erows[q] - left * erows[j]
                factors.append(m)
            for u in below:
                for j in range(8):
                    a[u] = a[u] - factors[j][u] * rows[j]
                    e[u] = e[u] - factors[j][u] * erows[j]
        for t in range(tiles):
            pivot = jnp.sum(jnp.where(lanes == subs + t * 8, a[t], 0.0), axis=1, keepdims=True)
            inverse[t * 8:(t + 1) * 8, :] = e[t] * (1.0 / jnp.sqrt(pivot))


    inverse = call(factor_of, sds((ncol, ncol), F32), in_specs=[VMEM()], micros=0.5)(after(sums, *image_all))

    def finish(*refs):
        full_ref, pieces, moments, inv_ref = refs[0], refs[1:1 + count], refs[1 + count:1 + 2 * count], refs[1 + 2 * count]
        basis_ref, image_ref, projected_ref, raw = refs[2 + 2 * count:]
        inv = inv_ref[...]
        turned = inv.T
        strips = [unpacked(moments, slice(0, span), g) for g in range(count)]
        m = jnp.concatenate(strips, axis=0) * (1.0 / total)
        half = exact(inv, m, ((1,), (0,)))
        for i in range(blk_dev):
            raw[i * blk:(i + 1) * blk, :] = unpacked(pieces, block_rows(i), i % count)
        basis_ref[...] = apply_wide(jnp.concatenate(split(full_ref[...]), axis=1), turned)
        image_ref[...] = apply_wide(jnp.concatenate(split(raw[...]), axis=1), turned)
        projected_ref[...] = exact(half, turned, ((1,), (0,)))

    return call(
        finish,
        (sds((rows_here, ncol), F32), sds((rows_here, ncol), F32), sds((ncol, ncol), F32)),
        in_specs=[VMEM()] * (2 + 2 * count),
        scratch=[pltpu.VMEM((rows_here, ncol), F32)],
        micros=3.0,
    )(full, *image_all, *moment_all, inverse)


def solution(mesh):
    in_specs = (
        P("rows", None),
        P("rows", None, None, None),
        P("rows", None, None),
        P("rows", None),
        P("rows", None),
    )
    out_specs = (P("rows", None), P("rows", None), P())
    return jax.shard_map(
        per_device, mesh=mesh, in_specs=in_specs, out_specs=out_specs, check_vma=False
    )
```
